128 devices in a mesh: ep: 4 (over x), edp: 32 (over z, y, core).
Axes of the slice: x: 4, y: 4, z: 4, core: 2. Of those that a mesh axis runs over, the one named last changes fastest.
Arguments:
- out_grad: bfloat16 [131072, 4096], P(('ep', 'edp')), may hold values from -6 to 6
- block_target: int32 [1024, 1], P(('ep', 'edp')), may hold values from 0 to 3; in each aligned block of 8 rows (0 to 7, 8 to 15, ...) at most 4 rows name the same one
- saved_hidden: bfloat16 [262144, 768], P(('ep', 'edp')), may hold values from -24 to 24
- master_weight: float32 [4, 768, 4096], P('ep', 'edp'), may hold values from -4 to 4
- first_moment: float32 [4, 768, 4096], P('ep', 'edp'), may hold values from -3 to 3
- second_moment: float32 [4, 768, 4096], P('ep', 'edp'), may hold values from 0.01 to 1
Outputs:
- hidden_grad: bfloat16 [131072, 768], P(('ep', 'edp'))
- new_weight: float32 [4, 768, 4096], P('ep', 'edp')
- new_first: float32 [4, 768, 4096], P('ep', 'edp')
- new_second: float32 [4, 768, 4096], P('ep', 'edp')
The draws below stay inside these ranges and needn't reach their ends.
Inputs may be any that keep to these rules, and one draw needn't show every extreme that they name: `block_target`: of one device's 8 blocks at most 4 go to one expert; in every draw some device sends exactly 4 blocks to some expert.
All inputs are finite; a program needn't handle non-finite values.
Results may differ from the reference program's by a relative error of at most 0.014.
Values may be sent and summed in bfloat16 or wider, within the bound.
A program may use at most 128 MiB of HBM per device.

```python
import math
import jax
import jax.numpy as jnp
import numpy as np
from jax import lax

D = 4096
FF = 768
BLOCK = 128
BLK_DEV = 8
CAP = 4
STEP = 1000
EXPERTS = 4
SLOTS = 2048
TOKENS = 131072
N_EP = 4
N_EDP = 32


def strengthened(drawn, key, source, target, shards_of, factor):
    owner, partner = [(jnp.arange(drawn.shape[dim]) // (drawn.shape[dim] // shards_of)).reshape([-1 if axis == dim else 1 for axis in range(drawn.ndim)]) for dim in (source, target)]
    chosen = jax.random.permutation(key, shards_of)[partner]
    strong = (owner == chosen) | (owner == (partner + shards_of // 2) % shards_of)
    return jnp.where(strong, factor * drawn, drawn)


def block_levels(stream_key, shape, shards, least, top_value):
    gain = 1.0
    for position, blocks in shards:
        steps = jax.random.uniform(jax.random.fold_in(jax.random.fold_in(stream_key, 6), position), (blocks,), jnp.float32, least / len(shards), top_value / len(shards))
        gain = gain * jnp.repeat(jnp.exp(steps), shape[position] // blocks).reshape((-1,) + (1,) * (len(shape) - 1 - position))
    return gain


def routed_block(key, own, number, rows, amount, top, bound, slope):
    order = jax.random.permutation(key, amount)
    crowded, usual = portions_of(amount, rows * top, bound, slope, True), portions_of(amount, rows * top, bound, slope, False)
    places = jnp.arange(amount)

    def named(tallies, turn):
        used = int((tallies > 0).sum())
        fixed = max(1, used // 4)
        passed = fixed + (places - fixed + turn * (used - fixed)) % max(1, amount - fixed)
        return jnp.zeros((amount,), jnp.int32).at[order[jnp.where(places < fixed, places, passed)]].set(jnp.asarray(tallies, jnp.int32))

    tallies = jnp.where(number % 4 == 0, named(crowded, number // 4), named(usual, number - number // 4 - 1))
    mixed = jax.random.permutation(jax.random.fold_in(own, 3), amount)
    donor, receiver = mixed[0:amount // 2 * 2:2], mixed[1:amount // 2 * 2:2]
    margin = jnp.minimum(tallies[donor] - 1, bound - tallies[receiver]) // 2
    margin = jnp.where((donor == order[0]) | (receiver == order[0]) | (tallies[receiver] == 0), 0, jnp.maximum(margin, 0))
    passed = jax.random.randint(jax.random.fold_in(own, 4), (amount // 2,), 0, 1 << 20) % (margin + 1)
    tallies = tallies.at[donor].add(-passed).at[receiver].add(passed)
    members = jnp.searchsorted(jnp.cumsum(tallies), jnp.arange(rows * top), side="right").astype(jnp.int32)
    grid = members.reshape(top, rows).T
    grid = grid[jax.random.permutation(jax.random.fold_in(own, 1), rows)]
    turn = jax.random.randint(jax.random.fold_in(own, 2), (rows, 1), 0, top)
    return jnp.take_along_axis(grid, (jnp.arange(top)[None, :] + turn) % top, axis=1)


def portions_of(number_of, total, most, lean, full):
    weights = [(1 << 20) // math.isqrt(rank ** lean) + 1 for rank in range(1, number_of + 1)]
    largest = most if full else min(most, max(-(-total // number_of), total * weights[0] // sum(weights)))
    least = 1 if total - largest >= number_of - 1 else 0
    counts, surplus = [largest] + [least] * (number_of - 1), total - largest - least * (number_of - 1)
    while surplus > 0:
        movable = [i for i in range(1, number_of) if counts[i] < largest] or [i for i in range(1, number_of) if counts[i] < most]
        mass, left = sum([weights[i] for i in movable]), surplus
        for i in movable:
            addition = min(most - counts[i], max(1, left * weights[i] // mass), surplus)
            counts[i] = counts[i] + addition
            surplus = surplus - addition
    return np.array(counts)


def scatter_about(stream_key, dims, scale, reach, split=(), held_as=jnp.bfloat16):
    drawn = scale * jax.random.normal(stream_key, dims, jnp.float32)
    if split:
        drawn = drawn * block_levels(stream_key, dims, split, -0.22, 0.18)
    return jnp.clip(drawn, -reach, reach).astype(held_as)


def heavy_noise(stream_key, extent, scale, most, split, heavy, kind=jnp.bfloat16):
    entries = scale * jax.random.normal(stream_key, extent, jnp.float32)
    if split:
        entries = entries * block_levels(stream_key, extent, split, -0.22, 0.18)
    return jnp.clip(strengthened(entries, jax.random.fold_in(stream_key, 3), *heavy), -most, most).astype(kind)


def setup_inputs(seed: int = 0) -> dict:
    splits = jax.random.split(jax.random.key(seed), 7)
    out_grad = scatter_about(splits[0], (TOKENS, D), 1.0, 6.0, ((0, 128),))
    block_target_keys = jax.random.split(jax.random.fold_in(splits[1], 1), (N_EP * N_EDP * BLK_DEV) // BLK_DEV)
    block_target_turns = jax.random.permutation(jax.random.fold_in(splits[1], 3), (N_EP * N_EDP * BLK_DEV) // BLK_DEV)
    block_target = jax.vmap(lambda own, number: routed_block(jax.random.fold_in(splits[1], 2), own, number, BLK_DEV, N_EP, 1, CAP, 2))(block_target_keys, block_target_turns).reshape((N_EP * N_EDP * BLK_DEV, 1))
    saved_hidden = heavy_noise(splits[2], (N_EP * N_EDP * SLOTS, FF), 1.0, 24.0, ((0, 128),), (0, 1, 128, 5.5))
    master_weight = scatter_about(splits[3], (EXPERTS, FF, D), 1.0, 4.0, ((0, 4), (1, 32)), jnp.float32)
    first_moment = scatter_about(splits[4], (EXPERTS, FF, D), 0.5, 3.0, ((0, 4), (1, 32)), jnp.float32)
    second_moment = jnp.clip(jnp.exp(math.log(1.0) - 4.6051702 * jax.random.uniform(splits[5], (EXPERTS, FF, D), jnp.float32) ** block_levels(splits[5], (EXPERTS, FF, D), ((0, 4), (1, 32)), -0.2, 0.2)), 0.01, 1.0)
    return {"out_grad": out_grad, "block_target": block_target, "saved_hidden": saved_hidden, "master_weight": master_weight, "first_moment": first_moment, "second_moment": second_moment}


BETA_ONE = 0.9
BETA_TWO = 0.999
LEARN_RATE = 0.01
EPSILON = 1e-08

def slot_ranks(targets):
    onehot = (targets[:, :, None] == jnp.arange(N_EP, dtype=jnp.int32)[None, None, :]).astype(jnp.int32)
    earlier = jnp.cumsum(onehot, axis=1) - onehot
    return lax.optimization_barrier(jnp.sum(earlier * onehot, axis=2)).astype(jnp.int32)

def reference(out_grad, block_target, saved_hidden, master_weight, first_moment, second_moment):
    all_devices = N_EP * N_EDP
    targets = block_target.reshape(all_devices, BLK_DEV).astype(jnp.int32)
    ranks = slot_ranks(targets)
    device_ids = jnp.arange(all_devices, dtype=jnp.int32)
    source_ep = (device_ids // N_EDP)[:, None]
    source_edp = (device_ids % N_EDP)[:, None]
    slot_ids = (((targets * N_EDP + source_edp) * N_EP + source_ep) * CAP + ranks).astype(jnp.int32)
    grad_blocks = out_grad.reshape(all_devices * BLK_DEV, BLOCK, D)
    weight_low = master_weight.astype(jnp.bfloat16)
    factor = D ** (-0.5)

    def visit(carry, inputs):
        block_rows, target, slot = inputs
        weight_now = lax.dynamic_index_in_dim(weight_low, target, 0, keepdims=False)
        back_rows = lax.dot_general(block_rows, weight_now, (((1,), (1,)), ((), ())), preferred_element_type=jnp.float32)
        hidden_rows = lax.dynamic_slice_in_dim(saved_hidden, (slot * BLOCK).astype(jnp.int32), BLOCK, 0)
        grad_term = lax.dot_general(hidden_rows, block_rows, (((0,), (0,)), ((), ())), preferred_element_type=jnp.float32)
        current = lax.dynamic_index_in_dim(carry, target, 0, keepdims=True)
        carry = lax.dynamic_update_index_in_dim(carry, current + grad_term[None], target, 0)
        return (carry, (back_rows * factor).astype(jnp.bfloat16))
    totals, hidden_back = lax.scan(visit, jnp.zeros((N_EP, FF, D), jnp.float32), (grad_blocks, targets.reshape(-1), slot_ids.reshape(-1)))
    weight_grad = totals * factor
    hidden_grad = hidden_back.reshape(all_devices * BLK_DEV * BLOCK, FF)
    new_first = BETA_ONE * first_moment + (1.0 - BETA_ONE) * weight_grad
    new_second = BETA_TWO * second_moment + (1.0 - BETA_TWO) * weight_grad * weight_grad
    first_fix = 1.0 - BETA_ONE ** STEP
    second_fix = 1.0 - BETA_TWO ** STEP
    new_weight = master_weight - LEARN_RATE * (new_first / first_fix) / (jnp.sqrt(new_second / second_fix) + EPSILON)
    return (hidden_grad, new_weight, new_first, new_second)
```

```python
import jax
import jax.numpy as jnp
from jax import lax
from jax.experimental import pallas as pl
from jax.experimental.pallas import tpu as pltpu
from jax.sharding import PartitionSpec as P

MESH = pl.DeviceIdType.MESH
F32 = jnp.float32
BF16 = jnp.bfloat16

BLOCK = 128
STEP = 1000
BETA_ONE = 0.9
BETA_TWO = 0.999
LEARN_RATE = 0.01
EPSILON = 1e-08

RING = 4
EXPERTS = 4
CAP = 4
BLOCKS = 8
D = 4096
HALF = D // 2
FF = 768
ROWS = 48
X, Z, Y = 0, 1, 2
GROUPS = ((512, (Y, Z, X)), (768, (X, Y, Z)), (768, (X, Z, Y)))
OFFSETS = (0, 512, 1280)
NG = len(GROUPS)
TILE = 256


def kernel(og_hbm, bt_ref, sh_hbm, mw_hbm, hg_hbm, wg_ref, *scratch):
    it = iter(scratch)
    og = next(it)
    w = [next(it) for _ in range(NG)]
    part = [next(it) for _ in range(NG)]
    land = [[next(it) for _ in range(3)] for _ in range(NG)]
    hid = next(it)
    fwd = next(it)
    hid_t = next(it)
    wbuf = next(it)
    tgt = next(it)
    tsm = next(it)
    hsend = next(it)
    hrecv = next(it)
    fin = next(it)
    wgs = next(it)
    ag_s, ag_r, rs_s, rs_r = next(it), next(it), next(it), next(it)
    hs, hr, hcs, hcr = next(it), next(it), next(it), next(it)
    ms, mr = next(it), next(it)
    loc = next(it)
    hps, hpr, hos = next(it), next(it), next(it)

    x = lax.axis_index("ep")
    e = lax.axis_index("edp")
    c = lax.rem(e, 2)
    y = lax.rem(e // 2, RING)
    z = e // (2 * RING)
    oc = 1 - c
    mine = (x, z, y)

    def wrap(v):
        return lax.rem(v + RING, RING)

    def near(axis, delta):
        at = list(mine)
        at[axis] = wrap(at[axis] + delta)
        return (at[0], (at[1] * RING + at[2]) * 2 + c)

    other = (x, e + 1 - 2 * c)

    barrier = pltpu.get_barrier_semaphore()
    for axis in (X, Z, Y):
        for delta in (1, -1):
            pl.semaphore_signal(barrier, inc=1, device_id=near(axis, delta), device_id_type=MESH)
    pl.semaphore_signal(barrier, inc=1, device_id=other, device_id_type=MESH)
    tgt[c] = jnp.broadcast_to(bt_ref[...], (BLOCKS, 128))
    pl.semaphore_wait(barrier, 7)

    sent = []

    def remote(src, dst, s, r, dev):
        return pltpu.make_async_remote_copy(
            src_ref=src, dst_ref=dst, send_sem=s, recv_sem=r, device_id=dev, device_id_type=MESH
        )

    def push(*a):
        copy = remote(*a)
        copy.start()
        sent.append(copy)
        return copy

    def cols(who):
        return pl.ds(pl.multiple_of(who * HALF, HALF), HALF)

    def seg(who, n, start=0):
        return pl.ds(pl.multiple_of(who * CAP * BLOCK, CAP * BLOCK) + start, n)

    w_local = pltpu.make_async_copy(mw_hbm.at[0, :, cols(c)], wbuf.at[c], loc.at[0])
    w_local.start()
    w_peer = push(mw_hbm.at[0, :, cols(oc)], wbuf.at[c], ms.at[0], mr.at[0], other)
    t_peer = push(tgt.at[c], tgt.at[c], ms.at[1], mr.at[1], other)
    SEGR = CAP * BLOCK
    HS = SEGR // 2
    for d, delta in enumerate((1, -1)):
        push(sh_hbm.at[seg(wrap(x + 2), HS, d * HS)], fwd.at[d], hs.at[d, 0], hr.at[d, 0], near(X, delta))
    for d, delta in enumerate((1, -1)):
        push(sh_hbm.at[seg(wrap(x + delta), SEGR)], hid.at[c, x], hs.at[d, 1], hr.at[d, 1], near(X, delta))
    h_local = pltpu.make_async_copy(sh_hbm.at[seg(x, SEGR)], hid.at[c, x], loc.at[1])
    h_local.start()

    def block(ref, g, p, q, h):
        width, order = GROUPS[g]
        at = list(mine)
        for axis in order[:p]:
            at[axis] = pl.ds(0, RING)
        at[order[p]] = q
        return ref.at[at[0], at[1], at[2], :, pl.ds(h * (width // 2), width // 2)]

    def ag_copy(g, p, d, k, q, h):
        ref = block(w[g], g, p, q, h)
        return remote(ref, ref, ag_s.at[g, p, d, k], ag_r.at[g, p, d, k], near(GROUPS[g][1][p], 1 - 2 * d))

    def ag_start(g, p):
        m = mine[GROUPS[g][1][p]]
        for k in range(2):
            for d in range(2):
                copy = ag_copy(g, p, d, k, m, k ^ d)
                copy.start()
                sent.append(copy)

    def ag_forward(g, p):
        m = mine[GROUPS[g][1][p]]
        for d in range(2):
            ag_copy(g, p, d, 0, wrap(m - 1 + 2 * d), d).wait_recv()
            copy = ag_copy(g, p, d, 2, wrap(m - 1 + 2 * d), d)
            copy.start()
            sent.append(copy)

    def ag_finish(g, p):
        m = mine[GROUPS[g][1][p]]
        for d in range(2):
            ag_copy(g, p, d, 1, wrap(m - 1 + 2 * d), 1 - d).wait_recv()
            ag_copy(g, p, d, 2, wrap(m + 2), d).wait_recv()

    w_local.wait()
    remote(mw_hbm.at[0, :, cols(c)], wbuf.at[oc], ms.at[0], mr.at[0], other).wait_recv()
    for g, (width, _) in enumerate(GROUPS):
        rows = wbuf[:, :, OFFSETS[g] : OFFSETS[g] + width].reshape(ROWS, width)
        w[g][x, z, y] = rows.astype(BF16)
    for g in range(NG):
        ag_start(g, 0)

    og_local = pltpu.make_async_copy(og_hbm.at[:, :, cols(c)], og.at[c], loc.at[2])
    og_local.start()
    push(og_hbm.at[:, :, cols(oc)], og.at[c], ms.at[2], mr.at[2], other)
    push(sh_hbm.at[seg(x, SEGR)], hid.at[c, x], hcs.at[0], hcr.at[0], other)

    for g in range(NG):
        ag_forward(g, 0)
    for g in range(NG):
        ag_finish(g, 0)
    for g in range(NG):
        ag_start(g, 1)

    for d, delta in enumerate((1, -1)):
        remote(fwd.at[d], fwd.at[d], hs.at[d, 0], hr.at[d, 0], near(X, delta)).wait_recv()
        push(
            fwd.at[d],
            hid.at[c, wrap(x - delta), pl.ds(d * HS, HS)],
            hs.at[d, 2],
            hr.at[d, 2],
            near(X, delta),
        )

    for g in range(NG):
        ag_forward(g, 1)
    for g in range(NG):
        ag_finish(g, 1)
    for g in range(NG):
        ag_start(g, 2)

    remote(tgt.at[oc], tgt.at[oc], ms.at[1], mr.at[1], other).wait_recv()
    t_smem = pltpu.make_async_copy(tgt, tsm, loc.at[3])
    t_smem.start()
    t_smem.wait()

    def weight_grad(t):
        slots = []
        for k in range(2):
            count = jnp.int32(0)
            index = [jnp.int32(0)] * CAP
            valid = [jnp.int32(0)] * CAP
            for b in range(BLOCKS):
                hit = (tsm[k, b, 0] == t).astype(jnp.int32)
                for r in range(CAP):
                    here = hit * (count == r).astype(jnp.int32)
                    index[r] = index[r] + b * here
                    valid[r] = valid[r] + here
                count = count + hit
            for r in range(CAP):
                slots.append((k, index[r]))
                rows = hid[k, t, r * BLOCK : (r + 1) * BLOCK, :].astype(F32) * valid[r].astype(F32)
                at = (k * CAP + r) * BLOCK
                hid_t[:, at : at + BLOCK] = rows.astype(BF16).T
        for g, (width, _) in enumerate(GROUPS):

            def tile(j, carry, g=g):
                start = pl.multiple_of(j * TILE, TILE)
                rhs = jnp.concatenate(
                    [og[k, i, :, pl.ds(OFFSETS[g] + start, TILE)] for k, i in slots], axis=0
                )
                out = jnp.dot(hid_t[...], rhs, preferred_element_type=F32)
                part[g][t, :, :, :, pl.ds(start, TILE)] = out.astype(BF16).reshape(RING, RING, ROWS, TILE)
                return carry

            lax.fori_loop(0, width // TILE, tile, 0)

    def hid_peer(k, t):
        remote(hid.at[oc, t], hid.at[oc, t], hcs.at[k], hcr.at[k], other).wait_recv()

    h_local.wait()
    og_local.wait()
    remote(og_hbm.at[:, :, cols(c)], og.at[oc], ms.at[2], mr.at[2], other).wait_recv()
    hid_peer(0, x)
    weight_grad(x)
    for k, d, delta in ((1, 1, 1), (3, 0, -1)):
        t = wrap(x + delta)
        remote(hid.at[c, t], hid.at[c, t], hs.at[d, 1], hr.at[d, 1], near(X, -delta)).wait_recv()
        push(hid.at[c, t], hid.at[c, t], hcs.at[k], hcr.at[k], other)
    for k, delta in ((1, 1), (3, -1)):
        t = wrap(x + delta)
        hid_peer(k, t)
        weight_grad(t)
    for g in range(NG):
        ag_forward(g, 2)
    t = wrap(x + 2)
    for d, delta in enumerate((1, -1)):
        ref = hid.at[c, t, pl.ds(d * HS, HS)]
        remote(ref, ref, hs.at[d, 2], hr.at[d, 2], near(X, delta)).wait_recv()
    push(hid.at[c, t], hid.at[c, t], hcs.at[2], hcr.at[2], other)
    hid_peer(2, t)
    weight_grad(t)

    def rs_copy(g, p, d, k, q, h):
        return remote(
            block(part[g], g, p, q, h),
            land[g][p].at[d, k],
            rs_s.at[g, p, d, k],
            rs_r.at[g, p, d, k],
            near(GROUPS[g][1][p], 1 - 2 * d),
        )

    def rs_send(*a):
        copy = rs_copy(*a)
        copy.start()
        sent.append(copy)

    def rs_start(g, p):
        m = mine[GROUPS[g][1][p]]
        for d in range(2):
            rs_send(g, p, d, 0, wrap(m + 2), d)
        for d in range(2):
            rs_send(g, p, d, 1, wrap(m + 1 - 2 * d), 1 - d)

    def add_in(g, p, q, h, parts):
        width, order = GROUPS[g]
        half = width // 2
        free = sorted(order[:p])
        span = pl.ds(h * half, half)

        def one(i, carry):
            lead = (i // RING, lax.rem(i, RING)) if p == 2 else ((i,) if p == 1 else ())
            at = list(mine)
            for axis, v in zip(free, lead):
                at[axis] = v
            at[order[p]] = q
            total = part[g][at[0], at[1], at[2], :, span].astype(F32)
            for d, k in parts:
                total = total + land[g][p][(d, k) + lead].astype(F32)
            if p == 0 and len(parts) == 2:
                fin[:, OFFSETS[g] + h * half : OFFSETS[g] + (h + 1) * half] = total
            else:
                part[g][at[0], at[1], at[2], :, span] = total.astype(BF16)
            return carry

        if p == 0:
            one(0, 0)
        else:
            lax.fori_loop(0, RING**p, one, 0)

    def rs_middle(g, p):
        m = mine[GROUPS[g][1][p]]
        for d in range(2):
            q = wrap(m + 1 - 2 * d)
            rs_copy(g, p, d, 0, q, d).wait_recv()
            add_in(g, p, q, d, ((d, 0),))
            rs_send(g, p, d, 2, q, d)

    def rs_finish(g, p):
        m = mine[GROUPS[g][1][p]]
        for k in (1, 2):
            for d in range(2):
                rs_copy(g, p, d, k, m, d if k == 2 else 1 - d).wait_recv()
        add_in(g, p, m, 0, ((0, 2), (1, 1)))
        add_in(g, p, m, 1, ((0, 1), (1, 2)))

    for g in range(NG):
        rs_start(g, 2)

    for g in range(NG):
        ag_finish(g, 2)

    def half_product(k, b):
        t = tsm[k, b, 0]
        acc = jnp.zeros((BLOCK, FF), F32)
        for g, (width, _) in enumerate(GROUPS):
            lhs = og[k, b, :, OFFSETS[g] : OFFSETS[g] + width]
            rhs = w[g][t].reshape(FF, width)
            acc = acc + lax.dot_general(lhs, rhs, (((1,), (1,)), ((), ())), preferred_element_type=F32)
        return acc

    def for_peer(b, carry):
        hsend[b] = half_product(oc, b).astype(BF16)
        remote(hsend.at[b], hrecv.at[b], hps.at[b], hpr.at[b], other).start()
        return carry

    lax.fori_loop(0, BLOCKS, for_peer, 0)
    for g in range(NG):
        rs_middle(g, 2)

    def for_me(b, carry):
        acc = half_product(c, b)
        remote(hsend.at[b], hrecv.at[b], hps.at[b], hpr.at[b], other).wait_recv()
        hrecv[b] = ((acc + hrecv[b].astype(F32)) * (D**-0.5)).astype(BF16)
        pltpu.make_async_copy(hrecv.at[b], hg_hbm.at[b], hos.at[b]).start()
        return carry

    lax.fori_loop(0, BLOCKS, for_me, 0)
    for g in range(NG):
        rs_finish(g, 2)
    for p in (1, 0):
        for g in range(NG):
            rs_start(g, p)
        for g in range(NG):
            rs_middle(g, p)
        for g in range(NG):
            rs_finish(g, p)

    def rows_of(who):
        return pl.ds(pl.multiple_of(who * (ROWS // 2), 8), ROWS // 2)

    push(fin.at[rows_of(oc)], wgs.at[:, cols(c)], ms.at[3], mr.at[3], other)
    wgs[:, cols(c)] = fin[rows_of(c), :]
    remote(fin.at[rows_of(c)], wgs.at[:, cols(oc)], ms.at[3], mr.at[3], other).wait_recv()
    wg_ref[...] = wgs[...]

    def drain(b, carry):
        remote(hsend.at[b], hrecv.at[b], hps.at[b], hpr.at[b], other).wait_send()
        pltpu.make_async_copy(hrecv.at[b], hg_hbm.at[b], hos.at[b]).wait()
        return carry

    lax.fori_loop(0, BLOCKS, drain, 0)
    for copy in sent:
        copy.wait_send()


def exchange(out_grad, block_target, saved_hidden, master_weight):
    scratch = [pltpu.VMEM((2, BLOCKS, BLOCK, HALF), BF16)]
    for _ in range(2):
        scratch += [pltpu.VMEM((RING, RING, RING, ROWS, width), BF16) for width, _ in GROUPS]
    for width, _ in GROUPS:
        scratch += [pltpu.VMEM((2, 3) + (RING,) * p + (ROWS, width // 2), BF16) for p in range(3)]
    dma = pltpu.SemaphoreType.DMA
    scratch += [
        pltpu.VMEM((2, EXPERTS, CAP * BLOCK, FF), BF16),
        pltpu.VMEM((2, CAP * BLOCK // 2, FF), BF16),
        pltpu.VMEM((FF, 2 * CAP * BLOCK), BF16),
        pltpu.VMEM((2, ROWS // 2, HALF), F32),
        pltpu.VMEM((2, BLOCKS, 128), jnp.int32),
        pltpu.SMEM((2, BLOCKS, 128), jnp.int32),
        pltpu.VMEM((BLOCKS, BLOCK, FF), BF16),
        pltpu.VMEM((BLOCKS, BLOCK, FF), BF16),
        pltpu.VMEM((ROWS, HALF), F32),
        pltpu.VMEM((ROWS // 2, D), F32),
        dma((NG, 3, 2, 3)),
        dma((NG, 3, 2, 3)),
        dma((NG, 3, 2, 3)),
        dma((NG, 3, 2, 3)),
        dma((2, 3)),
        dma((2, 3)),
        dma((4,)),
        dma((4,)),
        dma((4,)),
        dma((4,)),
        dma((4,)),
        dma((BLOCKS,)),
        dma((BLOCKS,)),
        dma((BLOCKS,)),
    ]
    anywhere = pl.BlockSpec(memory_space=pl.ANY)
    return pl.pallas_call(
        kernel,
        out_shape=(
            jax.ShapeDtypeStruct((BLOCKS, BLOCK, FF), BF16),
            jax.ShapeDtypeStruct((ROWS // 2, D), F32),
        ),
        in_specs=[anywhere, pl.BlockSpec(memory_space=pltpu.VMEM), anywhere, anywhere],
        out_specs=(anywhere, pl.BlockSpec(memory_space=pltpu.VMEM)),
        scratch_shapes=scratch,
        compiler_params=pltpu.CompilerParams(
            collective_id=0, has_side_effects=True, vmem_limit_bytes=63 * 1024 * 1024
        ),
        cost_estimate=pl.CostEstimate(flops=20 * 10**9, bytes_accessed=16 * 2**20, transcendentals=0),
    )(out_grad.reshape(BLOCKS, BLOCK, D), block_target, saved_hidden, master_weight)


def body(out_grad, block_target, saved_hidden, master_weight, first_moment, second_moment):
    hidden, total = exchange(out_grad, block_target, saved_hidden, master_weight)
    hidden_grad = hidden.reshape(BLOCKS * BLOCK, FF)
    weight_grad = total[None] * (D**-0.5)
    new_first = BETA_ONE * first_moment + (1.0 - BETA_ONE) * weight_grad
    new_second = BETA_TWO * second_moment + (1.0 - BETA_TWO) * weight_grad * weight_grad
    first_fix = 1.0 - BETA_ONE**STEP
    second_fix = 1.0 - BETA_TWO**STEP
    new_weight = master_weight - LEARN_RATE * (new_first / first_fix) / (
        jnp.sqrt(new_second / second_fix) + EPSILON
    )
    return (hidden_grad, new_weight, new_first, new_second)


def solution(mesh):
    rows = P(("ep", "edp"), None)
    shard = P("ep", "edp", None)
    return jax.shard_map(
        body,
        mesh=mesh,
        in_specs=(rows, rows, rows, shard, shard, shard),
        out_specs=(rows, shard, shard, shard),
        check_vma=False,
    )
```

```python
import jax
import jax.numpy as jnp
from jax import lax
from jax.experimental import pallas as pl
from jax.experimental.pallas import tpu as pltpu
from jax.sharding import PartitionSpec as P

MESH = pl.DeviceIdType.MESH
F32 = jnp.float32
BF16 = jnp.bfloat16

BLOCK = 128
STEP = 1000
BETA_ONE = 0.9
BETA_TWO = 0.999
LEARN_RATE = 0.01
EPSILON = 1e-08

RING = 4
EXPERTS = 4
CAP = 4
BLOCKS = 8
D = 4096
HALF = D // 2
FF = 768
ROWS = 48
X, Z, Y = 0, 1, 2
GROUPS = ((256, (X, Z, Y)), (256, (X, Y, Z)), (512, (X, Z, Y)), (512, (X, Y, Z)), (512, (Y, Z, X)))
OFFSETS = (0, 256, 512, 1024, 1536)
NG = len(GROUPS)
TILE = 256
UNIT = 4

ORDER = (
    ("as", 0, 0), ("as", 1, 0), ("as", 2, 0), ("as", 3, 0), ("as", 4, 0), ("a2a",), ("as", 0, 1), ("as", 1, 1),
    ("as", 4, 1), ("af", 0, 1), ("as", 2, 1), ("af", 1, 1), ("as", 3, 1), ("af", 4, 1), ("ht", 0), ("as", 1, 2),
    ("wg", 0, 0), ("wg", 0, 1), ("wg", 0, 2), ("as", 0, 2), ("af", 3, 1), ("wg", 0, 3), ("wg", 0, 4), ("af", 2, 1),
    ("as", 4, 2), ("af", 0, 2), ("af", 1, 2), ("as", 3, 2), ("hp", 1), ("hp", 3), ("ht", 1), ("as", 2, 2),
    ("ae", 0, 2), ("wg", 1, 0), ("wg", 1, 1), ("wg", 1, 2), ("wg", 1, 3), ("wg", 1, 4), ("ae", 1, 2), ("ht", 3),
    ("wg", 3, 0), ("wg", 3, 1), ("wg", 3, 2), ("wg", 3, 3), ("wg", 3, 4), ("af", 2, 2), ("af", 3, 2), ("hp", 2),
    ("ht", 2), ("wg", 2, 0), ("rs", 0, 2), ("wg", 2, 1), ("rs", 1, 2), ("wg", 2, 2), ("rs", 2, 2), ("wg", 2, 3),
    ("rs", 3, 2), ("wg", 2, 4), ("af", 4, 2), ("rs", 4, 2), ("ae", 2, 2), ("ae", 3, 2), ("rm", 0, 2), ("rm", 1, 2),
    ("ae", 4, 2), ("hg", 0), ("hg", 1), ("rm", 2, 2), ("rm", 3, 2), ("rm", 4, 2), ("hg", 2), ("hg", 3), ("rs", 0, 1),
    ("rs", 1, 1), ("rs", 4, 1), ("rm", 1, 1), ("rs", 2, 1), ("rm", 0, 1), ("rs", 1, 0), ("rs", 3, 1), ("rm", 2, 1),
    ("rm", 4, 1), ("re", 1, 0), ("rs", 0, 0), ("rm", 3, 1), ("rs", 2, 0), ("re", 0, 0), ("rs", 4, 0), ("rs", 3, 0),
    ("re", 2, 0), ("re", 4, 0), ("re", 3, 0),
)


def kernel(og_hbm, bt_hbm, sh_hbm, mw_hbm, hg_hbm, wg_ref, *scratch):
    it = iter(scratch)
    bt_ref = next(it)
    og = next(it)
    w = [next(it) for _ in range(NG)]
    part = [next(it) for _ in range(NG)]
    land = [[next(it) for _ in range(3)] for _ in range(NG)]
    hid = next(it)
    hid_t = next(it)
    wbuf = next(it)
    tgt = next(it)
    tsm = next(it)
    hsend = next(it)
    hrecv = next(it)
    fin = next(it)
    wgs = next(it)
    ag_s, ag_r, rs_s, rs_r = next(it), next(it), next(it), next(it)
    hs, hr, hcs, hcr = next(it), next(it), next(it), next(it)
    ms, mr = next(it), next(it)
    loc = next(it)
    hps, hpr, hos = next(it), next(it), next(it)

    x = lax.axis_index("ep")
    e = lax.axis_index("edp")
    c = lax.rem(e, 2)
    y = lax.rem(e // 2, RING)
    z = e // (2 * RING)
    oc = 1 - c
    mine = (x, z, y)

    def wrap(v):
        return lax.rem(v + RING, RING)

    def near(axis, delta):
        at = list(mine)
        at[axis] = wrap(at[axis] + delta)
        return (at[0], (at[1] * RING + at[2]) * 2 + c)

    other = (x, e + 1 - 2 * c)

    barrier = pltpu.get_barrier_semaphore()
    peers = [near(axis, delta) for axis in (X, Z, Y) for delta in (1, -1)]
    peers += [near(axis, 2) for axis in sorted({X} | {order[0] for _, order in GROUPS})] + [other]
    for peer in peers:
        pl.semaphore_signal(barrier, inc=1, device_id=peer, device_id_type=MESH)
    bt_local = pltpu.make_async_copy(bt_hbm, bt_ref, loc.at[4])
    bt_local.start()
    pl.semaphore_wait(barrier, len(peers))

    sent = []

    def remote(src, dst, s, r, dev):
        return pltpu.make_async_remote_copy(
            src_ref=src, dst_ref=dst, send_sem=s, recv_sem=r, device_id=dev, device_id_type=MESH
        )

    def push(*a):
        copy = remote(*a)
        copy.start()
        sent.append(copy)
        return copy

    def cols(who):
        return pl.ds(pl.multiple_of(who * HALF, HALF), HALF)

    def seg(who, n):
        return pl.ds(pl.multiple_of(who * CAP * BLOCK, CAP * BLOCK), n)

    SEGR = CAP * BLOCK
    w_local = pltpu.make_async_copy(mw_hbm.at[0, :, cols(c)], wbuf.at[c], loc.at[0])
    w_local.start()
    w_peer = push(mw_hbm.at[0, :, cols(oc)], wbuf.at[c], ms.at[0], mr.at[0], other)
    h_local = pltpu.make_async_copy(sh_hbm.at[seg(x, SEGR)], hid.at[c, x], loc.at[1])
    h_local.start()
    bt_local.wait()
    tgt[c] = jnp.broadcast_to(bt_ref[...], (BLOCKS, 128))
    push(tgt.at[c], tgt.at[c], ms.at[1], mr.at[1], other)

    def a2a():
        for i, delta in enumerate((1, -1, 2)):
            push(sh_hbm.at[seg(wrap(x + delta), SEGR)], hid.at[c, x], hs.at[i], hr.at[i], near(X, delta))

    def hid_push(k):
        t = wrap(x + k)
        i = (None, 1, 2, 0)[k]
        remote(hid.at[c, t], hid.at[c, t], hs.at[i], hr.at[i], near(X, k)).wait_recv()
        push(hid.at[c, t], hid.at[c, t], hcs.at[k], hcr.at[k], other)

    def block(ref, g, p, q, h):
        width, order = GROUPS[g]
        at = list(mine)
        for axis in order[:p]:
            at[axis] = pl.ds(0, RING)
        at[order[p]] = q
        if h is None:
            return ref.at[at[0], at[1], at[2]]
        return ref.at[at[0], at[1], at[2], :, pl.ds(h * (width // 2), width // 2)]

    def ag_copy(g, p, d, k, q, h):
        ref = block(w[g], g, p, q, h)
        return remote(ref, ref, ag_s.at[g, p, d, k], ag_r.at[g, p, d, k], near(GROUPS[g][1][p], 1 - 2 * d))

    DELTAS = (1, -1, 2)

    def ag_direct(g, k, q):
        ref = block(w[g], g, 0, q, None)
        return remote(ref, ref, ag_s.at[g, 0, 0, k], ag_r.at[g, 0, 0, k], near(GROUPS[g][1][0], DELTAS[k]))

    def ag_start(g, p):
        m = mine[GROUPS[g][1][p]]
        if p == 0:
            for k in range(3):
                copy = ag_direct(g, k, m)
                copy.start()
                sent.append(copy)
            return
        ag_finish(g, p - 1)
        for k in range(2):
            for d in range(2):
                copy = ag_copy(g, p, d, k, m, k ^ d)
                copy.start()
                sent.append(copy)

    def ag_forward(g, p):
        m = mine[GROUPS[g][1][p]]
        for d in range(2):
            ag_copy(g, p, d, 0, wrap(m - 1 + 2 * d), d).wait_recv()
            copy = ag_copy(g, p, d, 2, wrap(m - 1 + 2 * d), d)
            copy.start()
            sent.append(copy)

    def ag_finish(g, p):
        m = mine[GROUPS[g][1][p]]
        if p == 0:
            for k in range(3):
                ag_direct(g, k, wrap(m - DELTAS[k])).wait_recv()
            return
        for d in range(2):
            ag_copy(g, p, d, 1, wrap(m - 1 + 2 * d), 1 - d).wait_recv()
            ag_copy(g, p, d, 2, wrap(m + 2), d).wait_recv()

    w_local.wait()
    remote(mw_hbm.at[0, :, cols(c)], wbuf.at[oc], ms.at[0], mr.at[0], other).wait_recv()
    for g, (width, _) in enumerate(GROUPS):
        rows = wbuf[:, :, OFFSETS[g] : OFFSETS[g] + width].reshape(ROWS, width)
        w[g][x, z, y] = rows.astype(BF16)

    og_local = pltpu.make_async_copy(og_hbm.at[:, :, cols(c)], og.at[c], loc.at[2])
    og_local.start()
    push(og_hbm.at[:, :, cols(oc)], og.at[c], ms.at[2], mr.at[2], other)
    push(sh_hbm.at[seg(x, SEGR)], hid.at[c, x], hcs.at[0], hcr.at[0], other)

    slots = {}

    def take(k):
        t = wrap(x + k)
        if k == 0:
            remote(tgt.at[oc], tgt.at[oc], ms.at[1], mr.at[1], other).wait_recv()
            t_smem = pltpu.make_async_copy(tgt, tsm, loc.at[3])
            t_smem.start()
            t_smem.wait()
            h_local.wait()
            og_local.wait()
            remote(og_hbm.at[:, :, cols(c)], og.at[oc], ms.at[2], mr.at[2], other).wait_recv()
        remote(hid.at[oc, t], hid.at[oc, t], hcs.at[k], hcr.at[k], other).wait_recv()
        slots[k] = []
        for core in range(2):
            count = jnp.int32(0)
            index = [jnp.int32(0)] * CAP
            valid = [jnp.int32(0)] * CAP
            for b in range(BLOCKS):
                hit = (tsm[core, b, 0] == t).astype(jnp.int32)
                for r in range(CAP):
                    here = hit * (count == r).astype(jnp.int32)
                    index[r] = index[r] + b * here
                    valid[r] = valid[r] + here
                count = count + hit
            for r in range(CAP):
                slots[k].append((core, index[r]))
                rows = hid[core, t, r * BLOCK : (r + 1) * BLOCK, :].astype(F32) * valid[r].astype(F32)
                at = (core * CAP + r) * BLOCK
                hid_t[:, at : at + BLOCK] = rows.astype(BF16).T

    def weight_grad(k, g):
        t = wrap(x + k)
        width = GROUPS[g][0]

        def tile(j, carry):
            start = pl.multiple_of(j * TILE, TILE)
            rhs = jnp.concatenate(
                [og[core, i, :, pl.ds(OFFSETS[g] + start, TILE)] for core, i in slots[k]], axis=0
            )
            out = jnp.dot(hid_t[...], rhs, preferred_element_type=F32)
            part[g][t, :, :, :, pl.ds(start, TILE)] = out.astype(BF16).reshape(RING, RING, ROWS, TILE)
            return carry

        lax.fori_loop(0, width // TILE, tile, 0)

    def rs_copy(g, p, d, k, q, h):
        return remote(
            block(part[g], g, p, q, h),
            land[g][p].at[d, k],
            rs_s.at[g, p, d, k],
            rs_r.at[g, p, d, k],
            near(GROUPS[g][1][p], 1 - 2 * d),
        )

    def rs_send(*a):
        copy = rs_copy(*a)
        copy.start()
        sent.append(copy)

    def rs_direct(g, k, q):
        return remote(
            block(part[g], g, 0, q, None),
            land[g][0].at[k],
            rs_s.at[g, 0, 0, k],
            rs_r.at[g, 0, 0, k],
            near(GROUPS[g][1][0], DELTAS[k]),
        )

    def rs_start(g, p):
        m = mine[GROUPS[g][1][p]]
        if p < 2:
            rs_finish(g, p + 1)
        if p == 0:
            for k in range(3):
                copy = rs_direct(g, k, wrap(m + DELTAS[k]))
                copy.start()
                sent.append(copy)
            return
        for d in range(2):
            rs_send(g, p, d, 0, wrap(m + 2), d)
        for d in range(2):
            rs_send(g, p, d, 1, wrap(m + 1 - 2 * d), 1 - d)

    def add_in(g, p, q, h, parts):
        width, order = GROUPS[g]
        half = width // 2
        free = sorted(order[:p])
        span = pl.ds(h * half, half)

        def one(i, carry):
            lead = (i // RING, lax.rem(i, RING)) if p == 2 else (i,)
            at = list(mine)
            for axis, v in zip(free, lead):
                at[axis] = v
            at[order[p]] = q
            total = part[g][at[0], at[1], at[2], :, span].astype(F32)
            for d, k in parts:
                total = total + land[g][p][(d, k) + lead].astype(F32)
            part[g][at[0], at[1], at[2], :, span] = total.astype(BF16)
            return carry

        lax.fori_loop(0, RING**p, one, 0)

    def rs_middle(g, p):
        m = mine[GROUPS[g][1][p]]
        for d in range(2):
            q = wrap(m + 1 - 2 * d)
            rs_copy(g, p, d, 0, q, d).wait_recv()
            add_in(g, p, q, d, ((d, 0),))
            rs_send(g, p, d, 2, q, d)

    def rs_finish(g, p):
        m = mine[GROUPS[g][1][p]]
        if p == 0:
            total = part[g][mine].astype(F32)
            for k in range(3):
                rs_direct(g, k, m).wait_recv()
                total = total + land[g][0][k].astype(F32)
            fin[:, OFFSETS[g] : OFFSETS[g] + GROUPS[g][0]] = total
            return
        for k in (1, 2):
            for d in range(2):
                rs_copy(g, p, d, k, m, d if k == 2 else 1 - d).wait_recv()
        add_in(g, p, m, 0, ((0, 2), (1, 1)))
        add_in(g, p, m, 1, ((0, 1), (1, 2)))

    def half_product(k, b):
        t = tsm[k, b, 0]
        acc = jnp.zeros((BLOCK, FF), F32)
        for g, (width, _) in enumerate(GROUPS):
            lhs = og[k, b, :, OFFSETS[g] : OFFSETS[g] + width]
            rhs = w[g][t].reshape(FF, width)
            acc = acc + lax.dot_general(lhs, rhs, (((1,), (1,)), ((), ())), preferred_element_type=F32)
        return acc

    def for_peer(b, carry):
        hsend[b] = half_product(oc, b).astype(BF16)
        remote(hsend.at[b], hrecv.at[b], hps.at[b], hpr.at[b], other).start()
        return carry

    def for_me(b, carry):
        acc = half_product(c, b)
        remote(hsend.at[b], hrecv.at[b], hps.at[b], hpr.at[b], other).wait_recv()
        hrecv[b] = ((acc + hrecv[b].astype(F32)) * (D**-0.5)).astype(BF16)
        pltpu.make_async_copy(hrecv.at[b], hg_hbm.at[b], hos.at[b]).start()
        return carry

    def hidden_grad(u):
        start = u * UNIT
        if start < BLOCKS:
            lax.fori_loop(start, start + UNIT, for_peer, 0)
        else:
            lax.fori_loop(start - BLOCKS, start - BLOCKS + UNIT, for_me, 0)

    steps = {
        "as": ag_start,
        "af": ag_forward,
        "ae": ag_finish,
        "a2a": a2a,
        "hp": hid_push,
        "ht": take,
        "wg": weight_grad,
        "rs": rs_start,
        "rm": rs_middle,
        "re": rs_finish,
        "hg": hidden_grad,
    }
    for name, *where in ORDER:
        steps[name](*where)

    def rows_of(who):
        return pl.ds(pl.multiple_of(who * (ROWS // 2), 8), ROWS // 2)

    push(fin.at[rows_of(oc)], wgs.at[:, cols(c)], ms.at[3], mr.at[3], other)
    wgs[:, cols(c)] = fin[rows_of(c), :]
    remote(fin.at[rows_of(c)], wgs.at[:, cols(oc)], ms.at[3], mr.at[3], other).wait_recv()
    wg_ref[...] = wgs[...]

    def drain(b, carry):
        remote(hsend.at[b], hrecv.at[b], hps.at[b], hpr.at[b], other).wait_send()
        pltpu.make_async_copy(hrecv.at[b], hg_hbm.at[b], hos.at[b]).wait()
        return carry

    lax.fori_loop(0, BLOCKS, drain, 0)
    for copy in sent:
        copy.wait_send()


def exchange(out_grad, block_target, saved_hidden, master_weight):
    scratch = [pltpu.VMEM((BLOCKS, 1), jnp.int32), pltpu.VMEM((2, BLOCKS, BLOCK, HALF), BF16)]
    for _ in range(2):
        scratch += [pltpu.VMEM((RING, RING, RING, ROWS, width), BF16) for width, _ in GROUPS]
    for width, _ in GROUPS:
        scratch += [pltpu.VMEM((3, ROWS, width), BF16)]
        scratch += [pltpu.VMEM((2, 3) + (RING,) * p + (ROWS, width // 2), BF16) for p in (1, 2)]
    dma = pltpu.SemaphoreType.DMA
    scratch += [
        pltpu.VMEM((2, EXPERTS, CAP * BLOCK, FF), BF16),
        pltpu.VMEM((FF, 2 * CAP * BLOCK), BF16),
        pltpu.VMEM((2, ROWS // 2, HALF), F32),
        pltpu.VMEM((2, BLOCKS, 128), jnp.int32),
        pltpu.SMEM((2, BLOCKS, 128), jnp.int32),
        pltpu.VMEM((BLOCKS, BLOCK, FF), BF16),
        pltpu.VMEM((BLOCKS, BLOCK, FF), BF16),
        pltpu.VMEM((ROWS, HALF), F32),
        pltpu.VMEM((ROWS // 2, D), F32),
        dma((NG, 3, 2, 3)),
        dma((NG, 3, 2, 3)),
        dma((NG, 3, 2, 3)),
        dma((NG, 3, 2, 3)),
        dma((3,)),
        dma((3,)),
        dma((4,)),
        dma((4,)),
        dma((4,)),
        dma((4,)),
        dma((5,)),
        dma((BLOCKS,)),
        dma((BLOCKS,)),
        dma((BLOCKS,)),
    ]
    anywhere = pl.BlockSpec(memory_space=pl.ANY)
    return pl.pallas_call(
        kernel,
        out_shape=(
            jax.ShapeDtypeStruct((BLOCKS, BLOCK, FF), BF16),
            jax.ShapeDtypeStruct((ROWS // 2, D), F32),
        ),
        in_specs=[anywhere] * 4,
        out_specs=(anywhere, pl.BlockSpec(memory_space=pltpu.VMEM)),
        scratch_shapes=scratch,
        compiler_params=pltpu.CompilerParams(
            collective_id=0, has_side_effects=True, vmem_limit_bytes=63 * 1024 * 1024
        ),
        cost_estimate=pl.CostEstimate(flops=20 * 10**9, bytes_accessed=16 * 2**20, transcendentals=0),
    )(out_grad.reshape(BLOCKS, BLOCK, D), block_target, saved_hidden, master_weight)


def body(out_grad, block_target, saved_hidden, master_weight, first_moment, second_moment):
    hidden, total = exchange(out_grad, block_target, saved_hidden, master_weight)
    hidden_grad = hidden.reshape(BLOCKS * BLOCK, FF)
    weight_grad = total[None] * (D**-0.5)
    new_first = BETA_ONE * first_moment + (1.0 - BETA_ONE) * weight_grad
    new_second = BETA_TWO * second_moment + (1.0 - BETA_TWO) * weight_grad * weight_grad
    first_fix = 1.0 - BETA_ONE**STEP
    second_fix = 1.0 - BETA_TWO**STEP
    new_weight = master_weight - LEARN_RATE * (new_first / first_fix) / (
        jnp.sqrt(new_second / second_fix) + EPSILON
    )
    return (hidden_grad, new_weight, new_first, new_second)


def solution(mesh):
    rows = P(("ep", "edp"), None)
    shard = P("ep", "edp", None)
    return jax.shard_map(
        body,
        mesh=mesh,
        in_specs=(rows, rows, rows, shard, shard, shard),
        out_specs=(rows, shard, shard, shard),
        check_vma=False,
    )
```

```python
import jax
import jax.numpy as jnp
from jax import lax
from jax.experimental import pallas as pl
from jax.experimental.pallas import tpu as pltpu
from jax.sharding import PartitionSpec as P

MESH = pl.DeviceIdType.MESH
F32 = jnp.float32
BF16 = jnp.bfloat16

BLOCK = 128
STEP = 1000
BETA_ONE = 0.9
BETA_TWO = 0.999
LEARN_RATE = 0.01
EPSILON = 1e-08

RING = 4
EXPERTS = 4
CAP = 4
BLOCKS = 8
D = 4096
HALF = D // 2
FF = 768
ROWS = 48
X, Z, Y = 0, 1, 2
GROUPS = (
    (512, (X, Z, Y)),
    (512, (X, Y, Z)),
    (256, (X, Z, Y)),
    (256, (Y, Z, X)),
    (256, (X, Y, Z)),
    (256, (Z, Y, X)),
)
OFFSETS = (0, 512, 1024, 1280, 1536, 1792)
LATE = 1
NG = len(GROUPS)
TILE = 256
EARLY, UNIT = 2, 4

ORDER = (
    ("as", 3, 0), ("as", 4, 0), ("as", 2, 0), ("as", 5, 0), ("as", 0, 0), ("as", 3, 1), ("as", 4, 1), ("as", 1, 0),
    ("as", 2, 1), ("a2a", 0), ("af", 3, 1), ("as", 5, 1), ("ht", 0), ("af", 4, 1), ("af", 2, 1), ("as", 1, 1),
    ("wg", 0, 3), ("as", 0, 1), ("wg", 0, 5), ("as", 4, 2), ("wg", 0, 2), ("af", 1, 1), ("wg", 0, 0), ("af", 0, 1),
    ("as", 2, 2), ("wg", 0, 4), ("af", 4, 2), ("a2a", 1), ("af", 5, 1), ("af", 2, 2), ("wg", 0, 1), ("hp", 1),
    ("hp", 3), ("as", 1, 2), ("as", 0, 2), ("as", 3, 2), ("ht", 1), ("wg", 1, 4), ("wg", 1, 2), ("wg", 1, 0),
    ("wg", 1, 5), ("af", 0, 2), ("wg", 1, 1), ("wg", 1, 3), ("ht", 3), ("wg", 3, 0), ("wg", 3, 5), ("hp", 2),
    ("wg", 3, 2), ("af", 1, 2), ("wg", 3, 4), ("af", 3, 2), ("wg", 3, 3), ("wg", 3, 1), ("ht", 2), ("wg", 2, 5),
    ("wg", 2, 2), ("wg", 2, 1), ("rs", 1, 2), ("rs", 2, 2), ("ae", 4, 2), ("ae", 2, 2), ("wg", 2, 3), ("as", 5, 2),
    ("wg", 2, 0), ("wg", 2, 4), ("rs", 4, 2), ("ae", 1, 2), ("ae", 3, 2), ("rs", 0, 2), ("ae", 0, 2), ("ha", 0),
    ("ha", 1), ("af", 5, 2), ("rs", 3, 2), ("ha", 2), ("ha", 3), ("ha", 4), ("ha", 5), ("ae", 5, 2), ("ha", 6),
    ("ha", 7), ("rs", 5, 2), ("hb", 0), ("rm", 2, 2), ("hb", 1), ("rm", 1, 2), ("hb", 2), ("hb", 3), ("rm", 0, 2),
    ("rm", 3, 2), ("rm", 4, 2), ("rm", 5, 2), ("rs", 2, 1), ("rs", 1, 1), ("rs", 3, 1), ("rm", 2, 1), ("rs", 0, 1),
    ("rm", 1, 1), ("rs", 5, 1), ("rs", 4, 1), ("rm", 0, 1), ("rm", 3, 1), ("rs", 2, 0), ("rm", 5, 1), ("rs", 1, 0),
    ("rm", 4, 1), ("re", 2, 0), ("rs", 0, 0), ("rs", 5, 0), ("rs", 3, 0), ("re", 1, 0), ("rs", 4, 0), ("re", 5, 0),
    ("re", 3, 0), ("re", 0, 0), ("re", 4, 0),
)


def kernel(og_hbm, bt_hbm, sh_hbm, mw_hbm, hg_hbm, wg_ref, *scratch):
    it = iter(scratch)
    bt_ref = next(it)
    og = next(it)
    w = [next(it) for _ in range(NG)]
    part = [next(it) for _ in range(NG)]
    land = [[next(it) for _ in range(3)] for _ in range(NG)]
    hid = next(it)
    hid_t = next(it)
    wbuf = next(it)
    tgt = next(it)
    tsm = next(it)
    hsend = next(it)
    hrecv = next(it)
    acc = next(it)
    fin = next(it)
    wgs = next(it)
    ag_s, ag_r, rs_s, rs_r = next(it), next(it), next(it), next(it)
    hs, hr, hcs, hcr = next(it), next(it), next(it), next(it)
    ms, mr = next(it), next(it)
    loc = next(it)
    hps, hpr, hos = next(it), next(it), next(it)

    x = lax.axis_index("ep")
    e = lax.axis_index("edp")
    c = lax.rem(e, 2)
    y = lax.rem(e // 2, RING)
    z = e // (2 * RING)
    oc = 1 - c
    mine = (x, z, y)

    def wrap(v):
        return lax.rem(v + RING, RING)

    def near(axis, delta):
        at = list(mine)
        at[axis] = wrap(at[axis] + delta)
        return (at[0], (at[1] * RING + at[2]) * 2 + c)

    other = (x, e + 1 - 2 * c)

    barrier = pltpu.get_barrier_semaphore()
    peers = [near(axis, delta) for axis in (X, Z, Y) for delta in (1, -1)]
    peers += [near(axis, 2) for axis in sorted({X} | {order[0] for _, order in GROUPS})] + [other]
    for peer in peers:
        pl.semaphore_signal(barrier, inc=1, device_id=peer, device_id_type=MESH)

    def cols(who):
        return pl.ds(pl.multiple_of(who * HALF, HALF), HALF)

    def seg(who, n):
        return pl.ds(pl.multiple_of(who * CAP * BLOCK, CAP * BLOCK), n)

    SEGR = CAP * BLOCK
    w_local = pltpu.make_async_copy(mw_hbm.at[0, :, cols(c)], wbuf.at[c], loc.at[0])
    w_local.start()
    bt_local = pltpu.make_async_copy(bt_hbm, bt_ref, loc.at[4])
    bt_local.start()
    h_local = pltpu.make_async_copy(sh_hbm.at[seg(x, SEGR)], hid.at[c, x], loc.at[1])
    h_local.start()
    og_local = pltpu.make_async_copy(og_hbm.at[:, :, cols(c)], og.at[c], loc.at[2])
    og_local.start()
    pl.semaphore_wait(barrier, len(peers))

    sent = []

    def remote(src, dst, s, r, dev):
        return pltpu.make_async_remote_copy(
            src_ref=src, dst_ref=dst, send_sem=s, recv_sem=r, device_id=dev, device_id_type=MESH
        )

    def push(*a):
        copy = remote(*a)
        copy.start()
        sent.append(copy)
        return copy

    w_peer = push(mw_hbm.at[0, :, cols(oc)], wbuf.at[c], ms.at[0], mr.at[0], other)
    bt_local.wait()
    tgt[c] = jnp.zeros((BLOCKS, 128), jnp.int32)
    tgt[c, :, 0:BLOCKS] = jnp.broadcast_to(bt_ref[...], (BLOCKS, BLOCKS))
    push(tgt.at[c], tgt.at[c], ms.at[1], mr.at[1], other)

    def a2a(far):
        for i, delta in ((2, 2),) if far else ((0, 1), (1, -1)):
            push(sh_hbm.at[seg(wrap(x + delta), SEGR)], hid.at[c, x], hs.at[i], hr.at[i], near(X, delta))

    def hid_push(k):
        t = wrap(x + k)
        i = (None, 1, 2, 0)[k]
        remote(hid.at[c, t], hid.at[c, t], hs.at[i], hr.at[i], near(X, k)).wait_recv()
        push(hid.at[c, t], hid.at[c, t], hcs.at[k], hcr.at[k], other)

    def block(ref, g, p, q, h):
        width, order = GROUPS[g]
        at = list(mine)
        for axis in order[:p]:
            at[axis] = pl.ds(0, RING)
        at[order[p]] = q
        if h is None:
            return ref.at[at[0], at[1], at[2]]
        return ref.at[at[0], at[1], at[2], :, pl.ds(h * (width // 2), width // 2)]

    def ag_copy(g, p, d, k, q, h):
        ref = block(w[g], g, p, q, h)
        return remote(ref, ref, ag_s.at[g, p, d, k], ag_r.at[g, p, d, k], near(GROUPS[g][1][p], 1 - 2 * d))

    DELTAS = (1, -1, 2)

    def ag_direct(g, k, q):
        ref = block(w[g], g, 0, q, None)
        return remote(ref, ref, ag_s.at[g, 0, 0, k], ag_r.at[g, 0, 0, k], near(GROUPS[g][1][0], DELTAS[k]))

    def ag_start(g, p):
        m = mine[GROUPS[g][1][p]]
        if p == 0:
            for k in range(3):
                copy = ag_direct(g, k, m)
                copy.start()
                sent.append(copy)
            return
        ag_finish(g, p - 1)
        for k in range(2):
            for d in range(2):
                copy = ag_copy(g, p, d, k, m, k ^ d)
                copy.start()
                sent.append(copy)

    def ag_forward(g, p):
        m = mine[GROUPS[g][1][p]]
        for d in range(2):
            ag_copy(g, p, d, 0, wrap(m - 1 + 2 * d), d).wait_recv()
            copy = ag_copy(g, p, d, 2, wrap(m - 1 + 2 * d), d)
            copy.start()
            sent.append(copy)

    def ag_finish(g, p):
        m = mine[GROUPS[g][1][p]]
        if p == 0:
            for k in range(3):
                ag_direct(g, k, wrap(m - DELTAS[k])).wait_recv()
            return
        for d in range(2):
            ag_copy(g, p, d, 1, wrap(m - 1 + 2 * d), 1 - d).wait_recv()
            ag_copy(g, p, d, 2, wrap(m + 2), d).wait_recv()

    w_local.wait()
    remote(mw_hbm.at[0, :, cols(c)], wbuf.at[oc], ms.at[0], mr.at[0], other).wait_recv()
    for g, (width, _) in enumerate(GROUPS):
        rows = wbuf[:, :, OFFSETS[g] : OFFSETS[g] + width].reshape(ROWS, width)
        w[g][x, z, y] = rows.astype(BF16)
    push(og_hbm.at[:, :, cols(oc)], og.at[c], ms.at[2], mr.at[2], other)
    push(sh_hbm.at[seg(x, SEGR)], hid.at[c, x], hcs.at[0], hcr.at[0], other)

    slots = {}

    def take(k):
        t = wrap(x + k)
        if k == 0:
            remote(tgt.at[oc], tgt.at[oc], ms.at[1], mr.at[1], other).wait_recv()
            t_smem = pltpu.make_async_copy(tgt, tsm, loc.at[3])
            t_smem.start()
            t_smem.wait()
            h_local.wait()
            og_local.wait()
            remote(og_hbm.at[:, :, cols(c)], og.at[oc], ms.at[2], mr.at[2], other).wait_recv()
        remote(hid.at[oc, t], hid.at[oc, t], hcs.at[k], hcr.at[k], other).wait_recv()
        slots[k] = []
        for core in range(2):
            count = jnp.int32(0)
            index = [jnp.int32(0)] * CAP
            valid = [jnp.int32(0)] * CAP
            for b in range(BLOCKS):
                hit = (tsm[core, 0, b] == t).astype(jnp.int32)
                for r in range(CAP):
                    here = hit * (count == r).astype(jnp.int32)
                    index[r] = index[r] + b * here
                    valid[r] = valid[r] + here
                count = count + hit
            for r in range(CAP):
                slots[k].append((core, index[r]))
                rows = hid[core, t, r * BLOCK : (r + 1) * BLOCK, :].astype(F32) * valid[r].astype(F32)
                at = (core * CAP + r) * BLOCK
                hid_t[:, at : at + BLOCK] = rows.astype(BF16).T

    def weight_grad(k, g):
        t = wrap(x + k)
        width = GROUPS[g][0]

        def tile(j, carry):
            start = pl.multiple_of(j * TILE, TILE)
            rhs = jnp.concatenate(
                [og[core, i, :, pl.ds(OFFSETS[g] + start, TILE)] for core, i in slots[k]], axis=0
            )
            out = jnp.dot(hid_t[...], rhs, preferred_element_type=F32)
            part[g][t, :, :, :, pl.ds(start, TILE)] = out.astype(BF16).reshape(RING, RING, ROWS, TILE)
            return carry

        lax.fori_loop(0, width // TILE, tile, 0)

    def rs_copy(g, p, d, k, q, h):
        return remote(
            block(part[g], g, p, q, h),
            land[g][p].at[d, k],
            rs_s.at[g, p, d, k],
            rs_r.at[g, p, d, k],
            near(GROUPS[g][1][p], 1 - 2 * d),
        )

    def rs_send(*a):
        copy = rs_copy(*a)
        copy.start()
        sent.append(copy)

    def rs_direct(g, k, q):
        return remote(
            block(part[g], g, 0, q, None),
            land[g][0].at[k],
            rs_s.at[g, 0, 0, k],
            rs_r.at[g, 0, 0, k],
            near(GROUPS[g][1][0], DELTAS[k]),
        )

    def rs_start(g, p):
        m = mine[GROUPS[g][1][p]]
        if p < 2:
            rs_finish(g, p + 1)
        if p == 0:
            for k in range(3):
                copy = rs_direct(g, k, wrap(m + DELTAS[k]))
                copy.start()
                sent.append(copy)
            return
        for d in range(2):
            rs_send(g, p, d, 0, wrap(m + 2), d)
        for d in range(2):
            rs_send(g, p, d, 1, wrap(m + 1 - 2 * d), 1 - d)

    def add_in(g, p, q, h, parts):
        width, order = GROUPS[g]
        half = width // 2
        free = sorted(order[:p])
        span = pl.ds(h * half, half)

        def one(i, carry):
            lead = (i // RING, lax.rem(i, RING)) if p == 2 else (i,)
            at = list(mine)
            for axis, v in zip(free, lead):
                at[axis] = v
            at[order[p]] = q
            total = part[g][at[0], at[1], at[2], :, span].astype(F32)
            for d, k in parts:
                total = total + land[g][p][(d, k) + lead].astype(F32)
            part[g][at[0], at[1], at[2], :, span] = total.astype(BF16)
            return carry

        lax.fori_loop(0, RING**p, one, 0)

    def rs_middle(g, p):
        m = mine[GROUPS[g][1][p]]
        for d in range(2):
            q = wrap(m + 1 - 2 * d)
            rs_copy(g, p, d, 0, q, d).wait_recv()
            add_in(g, p, q, d, ((d, 0),))
            rs_send(g, p, d, 2, q, d)

    def rs_finish(g, p):
        m = mine[GROUPS[g][1][p]]
        if p == 0:
            total = part[g][mine].astype(F32)
            for k in range(3):
                rs_direct(g, k, m).wait_recv()
                total = total + land[g][0][k].astype(F32)
            fin[:, OFFSETS[g] : OFFSETS[g] + GROUPS[g][0]] = total
            return
        for k in (1, 2):
            for d in range(2):
                rs_copy(g, p, d, k, m, d if k == 2 else 1 - d).wait_recv()
        add_in(g, p, m, 0, ((0, 2), (1, 1)))
        add_in(g, p, m, 1, ((0, 1), (1, 2)))

    def half_product(k, b, groups):
        t = tsm[k, 0, b]
        acc = jnp.zeros((BLOCK, FF), F32)
        for g in groups:
            width = GROUPS[g][0]
            lhs = og[k, b, :, OFFSETS[g] : OFFSETS[g] + width]
            rhs = w[g][t].reshape(FF, width)
            acc = acc + lax.dot_general(lhs, rhs, (((1,), (1,)), ((), ())), preferred_element_type=F32)
        return acc

    def hidden_early(u):
        start = u * EARLY
        who, start = (oc, start) if start < BLOCKS else (c, start - BLOCKS)

        def one(b, carry):
            acc[who, b] = half_product(who, b, range(NG - LATE))
            return carry

        lax.fori_loop(start, start + EARLY, one, 0)

    def hidden_late(u):
        start = u * UNIT
        who, start = (oc, start) if start < BLOCKS else (c, start - BLOCKS)

        def one(b, carry):
            total = acc[who, b] + half_product(who, b, range(NG - LATE, NG))
            hop = remote(hsend.at[b], hrecv.at[b], hps.at[b], hpr.at[b], other)
            if u * UNIT < BLOCKS:
                hsend[b] = total.astype(BF16)
                hop.start()
            else:
                hop.wait_recv()
                hrecv[b] = ((total + hrecv[b].astype(F32)) * (D**-0.5)).astype(BF16)
                pltpu.make_async_copy(hrecv.at[b], hg_hbm.at[b], hos.at[b]).start()
            return carry

        lax.fori_loop(start, start + UNIT, one, 0)

    steps = {
        "as": ag_start,
        "af": ag_forward,
        "ae": ag_finish,
        "a2a": a2a,
        "hp": hid_push,
        "ht": take,
        "wg": weight_grad,
        "rs": rs_start,
        "rm": rs_middle,
        "re": rs_finish,
        "ha": hidden_early,
        "hb": hidden_late,
    }
    for name, *where in ORDER:
        steps[name](*where)

    def rows_of(who):
        return pl.ds(pl.multiple_of(who * (ROWS // 2), 8), ROWS // 2)

    push(fin.at[rows_of(oc)], wgs.at[:, cols(c)], ms.at[3], mr.at[3], other)
    wgs[:, cols(c)] = fin[rows_of(c), :]
    remote(fin.at[rows_of(c)], wgs.at[:, cols(oc)], ms.at[3], mr.at[3], other).wait_recv()
    wg_ref[...] = wgs[...]

    def drain(b, carry):
        remote(hsend.at[b], hrecv.at[b], hps.at[b], hpr.at[b], other).wait_send()
        pltpu.make_async_copy(hrecv.at[b], hg_hbm.at[b], hos.at[b]).wait()
        return carry

    lax.fori_loop(0, BLOCKS, drain, 0)
    for copy in sent:
        copy.wait_send()


def exchange(out_grad, block_target, saved_hidden, master_weight):
    scratch = [pltpu.VMEM((1, BLOCKS), jnp.int32), pltpu.VMEM((2, BLOCKS, BLOCK, HALF), BF16)]
    for _ in range(2):
        scratch += [pltpu.VMEM((RING, RING, RING, ROWS, width), BF16) for width, _ in GROUPS]
    for width, _ in GROUPS:
        scratch += [pltpu.VMEM((3, ROWS, width), BF16)]
        scratch += [pltpu.VMEM((2, 3) + (RING,) * p + (ROWS, width // 2), BF16) for p in (1, 2)]
    dma = pltpu.SemaphoreType.DMA
    scratch += [
        pltpu.VMEM((2, EXPERTS, CAP * BLOCK, FF), BF16),
        pltpu.VMEM((FF, 2 * CAP * BLOCK), BF16),
        pltpu.VMEM((2, ROWS // 2, HALF), F32),
        pltpu.VMEM((2, BLOCKS, 128), jnp.int32),
        pltpu.SMEM((2, BLOCKS, 128), jnp.int32),
        pltpu.VMEM((BLOCKS, BLOCK, FF), BF16),
        pltpu.VMEM((BLOCKS, BLOCK, FF), BF16),
        pltpu.VMEM((2, BLOCKS, BLOCK, FF), F32),
        pltpu.VMEM((ROWS, HALF), F32),
        pltpu.VMEM((ROWS // 2, D), F32),
        dma((NG, 3, 2, 3)),
        dma((NG, 3, 2, 3)),
        dma((NG, 3, 2, 3)),
        dma((NG, 3, 2, 3)),
        dma((3,)),
        dma((3,)),
        dma((4,)),
        dma((4,)),
        dma((4,)),
        dma((4,)),
        dma((5,)),
        dma((BLOCKS,)),
        dma((BLOCKS,)),
        dma((BLOCKS,)),
    ]
    anywhere = pl.BlockSpec(memory_space=pl.ANY)
    return pl.pallas_call(
        kernel,
        out_shape=(
            jax.ShapeDtypeStruct((BLOCKS, BLOCK, FF), BF16),
            jax.ShapeDtypeStruct((ROWS // 2, D), F32),
        ),
        in_specs=[anywhere] * 4,
        out_specs=(anywhere, pl.BlockSpec(memory_space=pltpu.VMEM)),
        scratch_shapes=scratch,
        compiler_params=pltpu.CompilerParams(
            collective_id=0, has_side_effects=True, vmem_limit_bytes=63 * 1024 * 1024
        ),
        cost_estimate=pl.CostEstimate(flops=20 * 10**9, bytes_accessed=16 * 2**20, transcendentals=0),
    )(out_grad.reshape(BLOCKS, BLOCK, D), block_target.reshape(1, BLOCKS), saved_hidden, master_weight)


def body(out_grad, block_target, saved_hidden, master_weight, first_moment, second_moment):
    hidden, total = exchange(out_grad, block_target, saved_hidden, master_weight)
    hidden_grad = hidden.reshape(BLOCKS * BLOCK, FF)
    weight_grad = total[None] * (D**-0.5)
    new_first = BETA_ONE * first_moment + (1.0 - BETA_ONE) * weight_grad
    new_second = BETA_TWO * second_moment + (1.0 - BETA_TWO) * weight_grad * weight_grad
    first_fix = 1.0 - BETA_ONE**STEP
    second_fix = 1.0 - BETA_TWO**STEP
    new_weight = master_weight - LEARN_RATE * (new_first / first_fix) / (
        jnp.sqrt(new_second / second_fix) + EPSILON
    )
    return (hidden_grad, new_weight, new_first, new_second)


def solution(mesh):
    rows = P(("ep", "edp"), None)
    shard = P("ep", "edp", None)
    return jax.shard_map(
        body,
        mesh=mesh,
        in_specs=(rows, rows, rows, shard, shard, shard),
        out_specs=(rows, shard, shard, shard),
        check_vma=False,
    )
```

```python
import jax
import jax.numpy as jnp
from jax import lax
from jax.experimental import pallas as pl
from jax.experimental.pallas import tpu as pltpu
from jax.sharding import PartitionSpec as P

MESH = pl.DeviceIdType.MESH
F32 = jnp.float32
BF16 = jnp.bfloat16

BLOCK = 128
STEP = 1000
BETA_ONE = 0.9
BETA_TWO = 0.999
LEARN_RATE = 0.01
EPSILON = 1e-08

RING = 4
EXPERTS = 4
CAP = 4
BLOCKS = 8
D = 4096
HALF = D // 2
FF = 768
ROWS = 48
X, Z, Y = 0, 1, 2
GROUPS = (
    (512, (X, Z, Y)),
    (512, (X, Y, Z)),
    (256, (X, Z, Y)),
    (256, (Y, Z, X)),
    (256, (X, Y, Z)),
    (256, (Z, Y, X)),
)
OFFSETS = (0, 512, 1024, 1280, 1536, 1792)
LATE = 1
NG = len(GROUPS)
TILE = 256
EARLY, UNIT = 2, 4

ORDER = (
    ("as", 4, 0), ("as", 3, 0), ("as", 0, 0), ("as", 5, 0), ("as", 2, 0), ("as", 1, 0), ("as", 4, 1), ("as", 3, 1),
    ("a2a", 0), ("as", 5, 1), ("as", 0, 1), ("af", 4, 1), ("ht", 0), ("as", 1, 1), ("a2a", 1), ("af", 3, 1),
    ("af", 0, 1), ("wg", 0, 3), ("af", 5, 1), ("as", 2, 1), ("wg", 0, 4), ("af", 1, 1), ("as", 4, 2), ("as", 0, 2),
    ("af", 2, 1), ("wg", 0, 0), ("wg", 0, 2), ("wg", 0, 1), ("as", 1, 2), ("hp", 1), ("as", 2, 2), ("wg", 0, 5),
    ("as", 3, 2), ("af", 0, 2), ("ht", 1), ("hp", 3), ("wg", 1, 2), ("wg", 1, 3), ("wg", 1, 1), ("wg", 1, 4),
    ("wg", 1, 5), ("wg", 1, 0), ("af", 2, 2), ("af", 1, 2), ("ht", 3), ("wg", 3, 3), ("wg", 3, 1), ("wg", 3, 2),
    ("af", 4, 2), ("hp", 2), ("wg", 3, 5), ("wg", 3, 0), ("wg", 3, 4), ("af", 3, 2), ("ht", 2), ("wg", 2, 4),
    ("wg", 2, 1), ("wg", 2, 0), ("wg", 2, 5), ("rs", 0, 2), ("rs", 1, 2), ("wg", 2, 2), ("rs", 4, 2), ("as", 5, 2),
    ("wg", 2, 3), ("ae", 2, 2), ("ae", 4, 2), ("ae", 3, 2), ("ae", 0, 2), ("ae", 1, 2), ("rs", 3, 2), ("ha", 0),
    ("ha", 1), ("ha", 2), ("ha", 3), ("af", 5, 2), ("rm", 0, 2), ("ha", 4), ("rs", 2, 2), ("ha", 5), ("rs", 5, 2),
    ("ha", 6), ("ha", 7), ("rm", 1, 2), ("ae", 5, 2), ("hb", 0), ("hb", 1), ("hb", 2), ("hb", 3), ("rm", 5, 2),
    ("rs", 0, 1), ("rm", 3, 2), ("rm", 2, 2), ("rm", 4, 2), ("rs", 1, 1), ("rm", 0, 1), ("rs", 5, 1), ("rs", 2, 1),
    ("rm", 1, 1), ("rs", 3, 1), ("rs", 4, 1), ("rs", 0, 0), ("rm", 2, 1), ("rm", 5, 1), ("rs", 1, 0), ("rm", 3, 1),
    ("rm", 4, 1), ("rs", 5, 0), ("rs", 2, 0), ("rs", 3, 0), ("rs", 4, 0), ("re", 0, 0), ("re", 5, 0), ("re", 2, 0),
    ("re", 1, 0), ("re", 3, 0), ("re", 4, 0),
)


def kernel(og_hbm, bt_hbm, sh_hbm, mw_hbm, hg_hbm, wg_ref, *scratch):
    it = iter(scratch)
    bt_ref = next(it)
    og = next(it)
    w = [next(it) for _ in range(NG)]
    part = [next(it) for _ in range(NG)]
    land = [[next(it) for _ in range(3)] for _ in range(NG)]
    hid = next(it)
    hid_t = next(it)
    wbuf = next(it)
    tgt = next(it)
    tsm = next(it)
    hsend = next(it)
    hrecv = next(it)
    acc = next(it)
    fin = next(it)
    wgs = next(it)
    ag_s, ag_r, rs_s, rs_r = next(it), next(it), next(it), next(it)
    hs, hr, hcs, hcr = next(it), next(it), next(it), next(it)
    ms, mr = next(it), next(it)
    loc = next(it)
    hps, hpr, hos = next(it), next(it), next(it)
    fs, fr = next(it), next(it)

    x = lax.axis_index("ep")
    e = lax.axis_index("edp")
    c = lax.rem(e, 2)
    y = lax.rem(e // 2, RING)
    z = e // (2 * RING)
    oc = 1 - c
    mine = (x, z, y)

    def wrap(v):
        return lax.rem(v + RING, RING)

    def near(axis, delta):
        at = list(mine)
        at[axis] = wrap(at[axis] + delta)
        return (at[0], (at[1] * RING + at[2]) * 2 + c)

    other = (x, e + 1 - 2 * c)

    barrier = pltpu.get_barrier_semaphore()
    peers = [near(axis, delta) for axis in (X, Z, Y) for delta in (1, -1)]
    peers += [near(axis, 2) for axis in sorted({X} | {order[0] for _, order in GROUPS})] + [other]
    for peer in peers:
        pl.semaphore_signal(barrier, inc=1, device_id=peer, device_id_type=MESH)

    def cols(who):
        return pl.ds(pl.multiple_of(who * HALF, HALF), HALF)

    def seg(who, n):
        return pl.ds(pl.multiple_of(who * CAP * BLOCK, CAP * BLOCK), n)

    SEGR = CAP * BLOCK
    w_local = pltpu.make_async_copy(mw_hbm.at[0, :, cols(c)], wbuf.at[c], loc.at[0])
    w_local.start()
    bt_local = pltpu.make_async_copy(bt_hbm, bt_ref, loc.at[4])
    bt_local.start()
    h_local = pltpu.make_async_copy(sh_hbm.at[seg(x, SEGR)], hid.at[c, x], loc.at[1])
    h_local.start()
    og_local = pltpu.make_async_copy(og_hbm.at[:, :, cols(c)], og.at[c], loc.at[2])
    og_local.start()
    pl.semaphore_wait(barrier, len(peers))

    sent = []

    def remote(src, dst, s, r, dev):
        return pltpu.make_async_remote_copy(
            src_ref=src, dst_ref=dst, send_sem=s, recv_sem=r, device_id=dev, device_id_type=MESH
        )

    def push(*a):
        copy = remote(*a)
        copy.start()
        sent.append(copy)
        return copy

    w_peer = push(mw_hbm.at[0, :, cols(oc)], wbuf.at[c], ms.at[0], mr.at[0], other)
    bt_local.wait()
    tgt[c] = jnp.zeros((BLOCKS, 128), jnp.int32)
    tgt[c, :, 0:BLOCKS] = jnp.broadcast_to(bt_ref[...], (BLOCKS, BLOCKS))
    push(tgt.at[c], tgt.at[c], ms.at[1], mr.at[1], other)

    def a2a(far):
        for i, delta in ((2, 2),) if far else ((0, 1), (1, -1)):
            push(sh_hbm.at[seg(wrap(x + delta), SEGR)], hid.at[c, x], hs.at[i], hr.at[i], near(X, delta))

    def hid_push(k):
        t = wrap(x + k)
        i = (None, 1, 2, 0)[k]
        remote(hid.at[c, t], hid.at[c, t], hs.at[i], hr.at[i], near(X, k)).wait_recv()
        push(hid.at[c, t], hid.at[c, t], hcs.at[k], hcr.at[k], other)

    def block(ref, g, p, q, h):
        width, order = GROUPS[g]
        at = list(mine)
        for axis in order[:p]:
            at[axis] = pl.ds(0, RING)
        at[order[p]] = q
        if h is None:
            return ref.at[at[0], at[1], at[2]]
        return ref.at[at[0], at[1], at[2], :, pl.ds(h * (width // 2), width // 2)]

    def ag_copy(g, p, d, k, q, h):
        ref = block(w[g], g, p, q, h)
        return remote(ref, ref, ag_s.at[g, p, d, k], ag_r.at[g, p, d, k], near(GROUPS[g][1][p], 1 - 2 * d))

    DELTAS = (1, -1, 2)

    def ag_direct(g, k, q):
        ref = block(w[g], g, 0, q, None)
        return remote(ref, ref, ag_s.at[g, 0, 0, k], ag_r.at[g, 0, 0, k], near(GROUPS[g][1][0], DELTAS[k]))

    def ag_start(g, p):
        m = mine[GROUPS[g][1][p]]
        if p == 0:
            for k in range(3):
                copy = ag_direct(g, k, m)
                copy.start()
                sent.append(copy)
            return
        ag_finish(g, p - 1)
        for k in range(2):
            for d in range(2):
                copy = ag_copy(g, p, d, k, m, k ^ d)
                copy.start()
                sent.append(copy)

    def ag_forward(g, p):
        m = mine[GROUPS[g][1][p]]
        for d in range(2):
            ag_copy(g, p, d, 0, wrap(m - 1 + 2 * d), d).wait_recv()
            copy = ag_copy(g, p, d, 2, wrap(m - 1 + 2 * d), d)
            copy.start()
            sent.append(copy)

    def ag_finish(g, p):
        m = mine[GROUPS[g][1][p]]
        if p == 0:
            for k in range(3):
                ag_direct(g, k, wrap(m - DELTAS[k])).wait_recv()
            return
        for d in range(2):
            ag_copy(g, p, d, 1, wrap(m - 1 + 2 * d), 1 - d).wait_recv()
            ag_copy(g, p, d, 2, wrap(m + 2), d).wait_recv()

    w_local.wait()
    remote(mw_hbm.at[0, :, cols(c)], wbuf.at[oc], ms.at[0], mr.at[0], other).wait_recv()
    for g, (width, _) in enumerate(GROUPS):
        rows = wbuf[:, :, OFFSETS[g] : OFFSETS[g] + width].reshape(ROWS, width)
        w[g][x, z, y] = rows.astype(BF16)
    push(og_hbm.at[:, :, cols(oc)], og.at[c], ms.at[2], mr.at[2], other)
    push(sh_hbm.at[seg(x, SEGR)], hid.at[c, x], hcs.at[0], hcr.at[0], other)

    slots = {}

    def take(k):
        t = wrap(x + k)
        if k == 0:
            remote(tgt.at[oc], tgt.at[oc], ms.at[1], mr.at[1], other).wait_recv()
            t_smem = pltpu.make_async_copy(tgt, tsm, loc.at[3])
            t_smem.start()
            t_smem.wait()
            h_local.wait()
            og_local.wait()
            remote(og_hbm.at[:, :, cols(c)], og.at[oc], ms.at[2], mr.at[2], other).wait_recv()
        remote(hid.at[oc, t], hid.at[oc, t], hcs.at[k], hcr.at[k], other).wait_recv()
        slots[k] = []
        for core in range(2):
            count = jnp.int32(0)
            index = [jnp.int32(0)] * CAP
            valid = [jnp.int32(0)] * CAP
            for b in range(BLOCKS):
                hit = (tsm[core, 0, b] == t).astype(jnp.int32)
                for r in range(CAP):
                    here = hit * (count == r).astype(jnp.int32)
                    index[r] = index[r] + b * here
                    valid[r] = valid[r] + here
                count = count + hit
            for r in range(CAP):
                slots[k].append((core, index[r]))
                rows = hid[core, t, r * BLOCK : (r + 1) * BLOCK, :].astype(F32) * valid[r].astype(F32)
                at = (core * CAP + r) * BLOCK
                hid_t[:, at : at + BLOCK] = rows.astype(BF16).T

    def weight_grad(k, g):
        t = wrap(x + k)
        width = GROUPS[g][0]

        def tile(j, carry):
            start = pl.multiple_of(j * TILE, TILE)
            rhs = jnp.concatenate(
                [og[core, i, :, pl.ds(OFFSETS[g] + start, TILE)] for core, i in slots[k]], axis=0
            )
            out = jnp.dot(hid_t[...], rhs, preferred_element_type=F32)
            part[g][t, :, :, :, pl.ds(start, TILE)] = out.astype(BF16).reshape(RING, RING, ROWS, TILE)
            return carry

        lax.fori_loop(0, width // TILE, tile, 0)

    def rows_of(who):
        return pl.ds(pl.multiple_of(who * (ROWS // 2), 8), ROWS // 2)

    def span_of(half, g):
        return pl.ds(pl.multiple_of(half * HALF, HALF) + OFFSETS[g], GROUPS[g][0])

    def fin_hop(g, half, rows):
        src = fin.at[rows_of(rows), OFFSETS[g] : OFFSETS[g] + GROUPS[g][0]]
        return (src, wgs.at[:, span_of(half, g)], fs.at[g], fr.at[g], other)

    def rs_copy(g, p, d, k, q, h):
        return remote(
            block(part[g], g, p, q, h),
            land[g][p].at[d, k],
            rs_s.at[g, p, d, k],
            rs_r.at[g, p, d, k],
            near(GROUPS[g][1][p], 1 - 2 * d),
        )

    def rs_send(*a):
        copy = rs_copy(*a)
        copy.start()
        sent.append(copy)

    def rs_direct(g, k, q):
        return remote(
            block(part[g], g, 0, q, None),
            land[g][0].at[k],
            rs_s.at[g, 0, 0, k],
            rs_r.at[g, 0, 0, k],
            near(GROUPS[g][1][0], DELTAS[k]),
        )

    def rs_start(g, p):
        m = mine[GROUPS[g][1][p]]
        if p < 2:
            rs_finish(g, p + 1)
        if p == 0:
            for k in range(3):
                copy = rs_direct(g, k, wrap(m + DELTAS[k]))
                copy.start()
                sent.append(copy)
            return
        for d in range(2):
            rs_send(g, p, d, 0, wrap(m + 2), d)
        for d in range(2):
            rs_send(g, p, d, 1, wrap(m + 1 - 2 * d), 1 - d)

    def add_in(g, p, q, h, parts):
        width, order = GROUPS[g]
        half = width // 2
        free = sorted(order[:p])
        span = pl.ds(h * half, half)

        def one(i, carry):
            lead = (i // RING, lax.rem(i, RING)) if p == 2 else (i,)
            at = list(mine)
            for axis, v in zip(free, lead):
                at[axis] = v
            at[order[p]] = q
            total = part[g][at[0], at[1], at[2], :, span].astype(F32)
            for d, k in parts:
                total = total + land[g][p][(d, k) + lead].astype(F32)
            part[g][at[0], at[1], at[2], :, span] = total.astype(BF16)
            return carry

        lax.fori_loop(0, RING**p, one, 0)

    def rs_middle(g, p):
        m = mine[GROUPS[g][1][p]]
        for d in range(2):
            q = wrap(m + 1 - 2 * d)
            rs_copy(g, p, d, 0, q, d).wait_recv()
            add_in(g, p, q, d, ((d, 0),))
            rs_send(g, p, d, 2, q, d)

    def rs_finish(g, p):
        m = mine[GROUPS[g][1][p]]
        if p == 0:
            total = part[g][mine].astype(F32)
            for k in range(3):
                rs_direct(g, k, m).wait_recv()
                total = total + land[g][0][k].astype(F32)
            fin[:, OFFSETS[g] : OFFSETS[g] + GROUPS[g][0]] = total
            push(*fin_hop(g, c, oc))
            wgs[:, span_of(c, g)] = fin[rows_of(c), OFFSETS[g] : OFFSETS[g] + GROUPS[g][0]]
            return
        for k in (1, 2):
            for d in range(2):
                rs_copy(g, p, d, k, m, d if k == 2 else 1 - d).wait_recv()
        add_in(g, p, m, 0, ((0, 2), (1, 1)))
        add_in(g, p, m, 1, ((0, 1), (1, 2)))

    def half_product(k, b, groups):
        t = tsm[k, 0, b]
        acc = jnp.zeros((BLOCK, FF), F32)
        for g in groups:
            width = GROUPS[g][0]
            lhs = og[k, b, :, OFFSETS[g] : OFFSETS[g] + width]
            rhs = w[g][t].reshape(FF, width)
            acc = acc + lax.dot_general(lhs, rhs, (((1,), (1,)), ((), ())), preferred_element_type=F32)
        return acc

    def hidden_early(u):
        start = u * EARLY
        who, start = (oc, start) if start < BLOCKS else (c, start - BLOCKS)

        def one(b, carry):
            acc[who, b] = half_product(who, b, range(NG - LATE))
            return carry

        lax.fori_loop(start, start + EARLY, one, 0)

    def hidden_late(u):
        start = u * UNIT
        who, start = (oc, start) if start < BLOCKS else (c, start - BLOCKS)

        def one(b, carry):
            total = acc[who, b] + half_product(who, b, range(NG - LATE, NG))
            hop = remote(hsend.at[b], hrecv.at[b], hps.at[b], hpr.at[b], other)
            if u * UNIT < BLOCKS:
                hsend[b] = total.astype(BF16)
                hop.start()
            else:
                hop.wait_recv()
                hrecv[b] = ((total + hrecv[b].astype(F32)) * (D**-0.5)).astype(BF16)
                pltpu.make_async_copy(hrecv.at[b], hg_hbm.at[b], hos.at[b]).start()
            return carry

        lax.fori_loop(start, start + UNIT, one, 0)

    steps = {
        "as": ag_start,
        "af": ag_forward,
        "ae": ag_finish,
        "a2a": a2a,
        "hp": hid_push,
        "ht": take,
        "wg": weight_grad,
        "rs": rs_start,
        "rm": rs_middle,
        "re": rs_finish,
        "ha": hidden_early,
        "hb": hidden_late,
    }
    for name, *where in ORDER:
        steps[name](*where)

    for g in range(NG):
        remote(*fin_hop(g, oc, c)).wait_recv()
    wg_ref[...] = wgs[...]

    def drain(b, carry):
        remote(hsend.at[b], hrecv.at[b], hps.at[b], hpr.at[b], other).wait_send()
        pltpu.make_async_copy(hrecv.at[b], hg_hbm.at[b], hos.at[b]).wait()
        return carry

    lax.fori_loop(0, BLOCKS, drain, 0)
    for copy in sent:
        copy.wait_send()


def exchange(out_grad, block_target, saved_hidden, master_weight):
    scratch = [pltpu.VMEM((1, BLOCKS), jnp.int32), pltpu.VMEM((2, BLOCKS, BLOCK, HALF), BF16)]
    for _ in range(2):
        scratch += [pltpu.VMEM((RING, RING, RING, ROWS, width), BF16) for width, _ in GROUPS]
    for width, _ in GROUPS:
        scratch += [pltpu.VMEM((3, ROWS, width), BF16)]
        scratch += [pltpu.VMEM((2, 3) + (RING,) * p + (ROWS, width // 2), BF16) for p in (1, 2)]
    dma = pltpu.SemaphoreType.DMA
    scratch += [
        pltpu.VMEM((2, EXPERTS, CAP * BLOCK, FF), BF16),
        pltpu.VMEM((FF, 2 * CAP * BLOCK), BF16),
        pltpu.VMEM((2, ROWS // 2, HALF), F32),
        pltpu.VMEM((2, BLOCKS, 128), jnp.int32),
        pltpu.SMEM((2, BLOCKS, 128), jnp.int32),
        pltpu.VMEM((BLOCKS, BLOCK, FF), BF16),
        pltpu.VMEM((BLOCKS, BLOCK, FF), BF16),
        pltpu.VMEM((2, BLOCKS, BLOCK, FF), F32),
        pltpu.VMEM((ROWS, HALF), F32),
        pltpu.VMEM((ROWS // 2, D), F32),
        dma((NG, 3, 2, 3)),
        dma((NG, 3, 2, 3)),
        dma((NG, 3, 2, 3)),
        dma((NG, 3, 2, 3)),
        dma((3,)),
        dma((3,)),
        dma((4,)),
        dma((4,)),
        dma((4,)),
        dma((4,)),
        dma((5,)),
        dma((BLOCKS,)),
        dma((BLOCKS,)),
        dma((BLOCKS,)),
        dma((NG,)),
        dma((NG,)),
    ]
    anywhere = pl.BlockSpec(memory_space=pl.ANY)
    return pl.pallas_call(
        kernel,
        out_shape=(
            jax.ShapeDtypeStruct((BLOCKS, BLOCK, FF), BF16),
            jax.ShapeDtypeStruct((ROWS // 2, D), F32),
        ),
        in_specs=[anywhere] * 4,
        out_specs=(anywhere, pl.BlockSpec(memory_space=pltpu.VMEM)),
        scratch_shapes=scratch,
        compiler_params=pltpu.CompilerParams(
            collective_id=0, has_side_effects=True, vmem_limit_bytes=63 * 1024 * 1024
        ),
        cost_estimate=pl.CostEstimate(flops=20 * 10**9, bytes_accessed=16 * 2**20, transcendentals=0),
    )(out_grad.reshape(BLOCKS, BLOCK, D), block_target.reshape(1, BLOCKS), saved_hidden, master_weight)


def body(out_grad, block_target, saved_hidden, master_weight, first_moment, second_moment):
    hidden, total = exchange(out_grad, block_target, saved_hidden, master_weight)
    hidden_grad = hidden.reshape(BLOCKS * BLOCK, FF)
    weight_grad = total[None] * (D**-0.5)
    new_first = BETA_ONE * first_moment + (1.0 - BETA_ONE) * weight_grad
    new_second = BETA_TWO * second_moment + (1.0 - BETA_TWO) * weight_grad * weight_grad
    first_fix = 1.0 - BETA_ONE**STEP
    second_fix = 1.0 - BETA_TWO**STEP
    new_weight = master_weight - LEARN_RATE * (new_first / first_fix) / (
        jnp.sqrt(new_second / second_fix) + EPSILON
    )
    return (hidden_grad, new_weight, new_first, new_second)


def solution(mesh):
    rows = P(("ep", "edp"), None)
    shard = P("ep", "edp", None)
    return jax.shard_map(
        body,
        mesh=mesh,
        in_specs=(rows, rows, rows, shard, shard, shard),
        out_specs=(rows, shard, shard, shard),
        check_vma=False,
    )
```

```python
import jax
import jax.numpy as jnp
from jax import lax
from jax.experimental import pallas as pl
from jax.experimental.pallas import tpu as pltpu
from jax.sharding import PartitionSpec as P

MESH = pl.DeviceIdType.MESH
F32 = jnp.float32
BF16 = jnp.bfloat16

BLOCK = 128
STEP = 1000
BETA_ONE = 0.9
BETA_TWO = 0.999
LEARN_RATE = 0.01
EPSILON = 1e-08

RING = 4
EXPERTS = 4
CAP = 4
BLOCKS = 8
D = 4096
HALF = D // 2
FF = 768
ROWS = 48
X, Z, Y = 0, 1, 2
GROUPS = (
    (512, (X, Z, Y)),
    (512, (X, Y, Z)),
    (256, (X, Z, Y)),
    (256, (Y, Z, X)),
    (256, (X, Y, Z)),
    (256, (Z, Y, X)),
)
OFFSETS = (0, 512, 1024, 1280, 1536, 1792)
LATE = 1
NG = len(GROUPS)
TILE = 256
EARLY, UNIT = 2, 4

ORDER = (
    ("as", 4, 0), ("as", 3, 0), ("as", 0, 0), ("as", 5, 0), ("as", 2, 0), ("as", 1, 0), ("as", 4, 1), ("as", 3, 1),
    ("a2a", 0), ("as", 5, 1), ("as", 0, 1), ("af", 4, 1), ("as", 1, 1), ("a2a", 1), ("af", 3, 1), ("af", 0, 1),
    ("af", 5, 1), ("as", 2, 1), ("af", 1, 1), ("as", 4, 2), ("as", 0, 2), ("af", 2, 1), ("as", 1, 2), ("ht", 0),
    ("wg", 0, 3), ("wg", 0, 4), ("wg", 0, 0), ("wg", 0, 2), ("wg", 0, 1), ("hp", 1), ("as", 2, 2), ("wg", 0, 5),
    ("as", 3, 2), ("af", 0, 2), ("ht", 1), ("hp", 3), ("wg", 1, 2), ("wg", 1, 3), ("wg", 1, 1), ("wg", 1, 4),
    ("wg", 1, 5), ("wg", 1, 0), ("af", 2, 2), ("af", 1, 2), ("ht", 3), ("wg", 3, 3), ("wg", 3, 1), ("wg", 3, 2),
    ("af", 4, 2), ("hp", 2), ("wg", 3, 5), ("wg", 3, 0), ("wg", 3, 4), ("af", 3, 2), ("ht", 2), ("wg", 2, 4),
    ("wg", 2, 1), ("wg", 2, 0), ("wg", 2, 5), ("rs", 0, 2), ("rs", 1, 2), ("wg", 2, 2), ("rs", 4, 2), ("as", 5, 2),
    ("wg", 2, 3), ("ae", 2, 2), ("ae", 4, 2), ("ae", 3, 2), ("ae", 0, 2), ("ae", 1, 2), ("rs", 3, 2), ("ha", 0),
    ("ha", 1), ("ha", 2), ("ha", 3), ("af", 5, 2), ("rm", 0, 2), ("ha", 4), ("rs", 2, 2), ("ha", 5), ("rs", 5, 2),
    ("ha", 6), ("ha", 7), ("rm", 1, 2), ("ae", 5, 2), ("hb", 0), ("hb", 1), ("hb", 2), ("hb", 3), ("rm", 5, 2),
    ("rs", 0, 1), ("rm", 3, 2), ("rm", 2, 2), ("rm", 4, 2), ("rs", 1, 1), ("rm", 0, 1), ("rs", 5, 1), ("rs", 2, 1),
    ("rm", 1, 1), ("rs", 3, 1), ("rs", 4, 1), ("rs", 0, 0), ("rm", 2, 1), ("rm", 5, 1), ("rs", 1, 0), ("rm", 3, 1),
    ("rm", 4, 1), ("rs", 5, 0), ("rs", 2, 0), ("rs", 3, 0), ("rs", 4, 0), ("re", 0, 0), ("re", 5, 0), ("re", 2, 0),
    ("re", 1, 0), ("re", 3, 0), ("re", 4, 0),
)


def kernel(og_hbm, bt_hbm, sh_hbm, mw_hbm, hg_hbm, wg_hbm, *scratch):
    it = iter(scratch)
    bt_ref = next(it)
    og = next(it)
    w = [next(it) for _ in range(NG)]
    part = [next(it) for _ in range(NG)]
    land = [[next(it) for _ in range(3)] for _ in range(NG)]
    hid = next(it)
    hid_t = next(it)
    wbuf = next(it)
    tgt = next(it)
    tsm = next(it)
    hsend = next(it)
    hrecv = next(it)
    acc = next(it)
    fin = next(it)
    wgs = next(it)
    ag_s, ag_r, rs_s, rs_r = next(it), next(it), next(it), next(it)
    hs, hr, hcs, hcr = next(it), next(it), next(it), next(it)
    ms, mr = next(it), next(it)
    loc = next(it)
    hps, hpr, hos = next(it), next(it), next(it)
    fs, fr, ws = next(it), next(it), next(it)

    x = lax.axis_index("ep")
    e = lax.axis_index("edp")
    c = lax.rem(e, 2)
    y = lax.rem(e // 2, RING)
    z = e // (2 * RING)
    oc = 1 - c
    mine = (x, z, y)

    def wrap(v):
        return lax.rem(v + RING, RING)

    def near(axis, delta):
        at = list(mine)
        at[axis] = wrap(at[axis] + delta)
        return (at[0], (at[1] * RING + at[2]) * 2 + c)

    other = (x, e + 1 - 2 * c)

    barrier = pltpu.get_barrier_semaphore()
    peers = [near(axis, delta) for axis in (X, Z, Y) for delta in (1, -1)]
    peers += [near(axis, 2) for axis in sorted({X} | {order[0] for _, order in GROUPS})] + [other]
    for peer in peers[::-1]:
        pl.semaphore_signal(barrier, inc=1, device_id=peer, device_id_type=MESH)

    def cols(who):
        return pl.ds(pl.multiple_of(who * HALF, HALF), HALF)

    def seg(who, n):
        return pl.ds(pl.multiple_of(who * CAP * BLOCK, CAP * BLOCK), n)

    SEGR = CAP * BLOCK
    w_local = pltpu.make_async_copy(mw_hbm.at[0, :, cols(c)], wbuf.at[c], loc.at[0])
    w_local.start()
    bt_local = pltpu.make_async_copy(bt_hbm, bt_ref, loc.at[4])
    bt_local.start()
    h_local = pltpu.make_async_copy(sh_hbm.at[seg(x, SEGR)], hid.at[c, x], loc.at[1])
    h_local.start()
    og_local = pltpu.make_async_copy(og_hbm.at[:, :, cols(c)], og.at[c], loc.at[2])
    og_local.start()
    pl.semaphore_wait(barrier, len(peers))

    sent = []

    def remote(src, dst, s, r, dev):
        return pltpu.make_async_remote_copy(
            src_ref=src, dst_ref=dst, send_sem=s, recv_sem=r, device_id=dev, device_id_type=MESH
        )

    def push(*a):
        copy = remote(*a)
        copy.start()
        sent.append(copy)
        return copy

    w_peer = push(mw_hbm.at[0, :, cols(oc)], wbuf.at[c], ms.at[0], mr.at[0], other)
    bt_local.wait()
    tgt[c] = jnp.zeros((BLOCKS, 128), jnp.int32)
    tgt[c, :, 0:BLOCKS] = jnp.broadcast_to(bt_ref[...], (BLOCKS, BLOCKS))
    push(tgt.at[c], tgt.at[c], ms.at[1], mr.at[1], other)

    def a2a(far):
        for i, delta in ((2, 2),) if far else ((0, 1), (1, -1)):
            push(sh_hbm.at[seg(wrap(x + delta), SEGR)], hid.at[c, x], hs.at[i], hr.at[i], near(X, delta))

    def hid_push(k):
        t = wrap(x + k)
        i = (None, 1, 2, 0)[k]
        remote(hid.at[c, t], hid.at[c, t], hs.at[i], hr.at[i], near(X, k)).wait_recv()
        push(hid.at[c, t], hid.at[c, t], hcs.at[k], hcr.at[k], other)

    def block(ref, g, p, q, h):
        width, order = GROUPS[g]
        at = list(mine)
        for axis in order[:p]:
            at[axis] = pl.ds(0, RING)
        at[order[p]] = q
        if h is None:
            return ref.at[at[0], at[1], at[2]]
        return ref.at[at[0], at[1], at[2], :, pl.ds(h * (width // 2), width // 2)]

    def ag_copy(g, p, d, k, q, h):
        ref = block(w[g], g, p, q, h)
        return remote(ref, ref, ag_s.at[g, p, d, k], ag_r.at[g, p, d, k], near(GROUPS[g][1][p], 1 - 2 * d))

    DELTAS = (1, -1, 2)

    def ag_direct(g, k, q):
        ref = block(w[g], g, 0, q, None)
        return remote(ref, ref, ag_s.at[g, 0, 0, k], ag_r.at[g, 0, 0, k], near(GROUPS[g][1][0], DELTAS[k]))

    def ag_start(g, p):
        m = mine[GROUPS[g][1][p]]
        if p == 0:
            for k in range(3):
                copy = ag_direct(g, k, m)
                copy.start()
                sent.append(copy)
            return
        ag_finish(g, p - 1)
        for k in range(2):
            for d in range(2):
                copy = ag_copy(g, p, d, k, m, k ^ d)
                copy.start()
                sent.append(copy)

    def ag_forward(g, p):
        m = mine[GROUPS[g][1][p]]
        for d in range(2):
            ag_copy(g, p, d, 0, wrap(m - 1 + 2 * d), d).wait_recv()
            copy = ag_copy(g, p, d, 2, wrap(m - 1 + 2 * d), d)
            copy.start()
            sent.append(copy)

    def ag_finish(g, p):
        m = mine[GROUPS[g][1][p]]
        if p == 0:
            for k in range(3):
                ag_direct(g, k, wrap(m - DELTAS[k])).wait_recv()
            return
        for d in range(2):
            ag_copy(g, p, d, 1, wrap(m - 1 + 2 * d), 1 - d).wait_recv()
            ag_copy(g, p, d, 2, wrap(m + 2), d).wait_recv()

    w_local.wait()
    remote(mw_hbm.at[0, :, cols(c)], wbuf.at[oc], ms.at[0], mr.at[0], other).wait_recv()
    for g, (width, _) in enumerate(GROUPS):
        rows = wbuf[:, :, OFFSETS[g] : OFFSETS[g] + width].reshape(ROWS, width)
        w[g][x, z, y] = rows.astype(BF16)
    push(og_hbm.at[:, :, cols(oc)], og.at[c], ms.at[2], mr.at[2], other)
    push(sh_hbm.at[seg(x, SEGR)], hid.at[c, x], hcs.at[0], hcr.at[0], other)

    slots = {}

    def take(k):
        t = wrap(x + k)
        if k == 0:
            remote(tgt.at[oc], tgt.at[oc], ms.at[1], mr.at[1], other).wait_recv()
            t_smem = pltpu.make_async_copy(tgt, tsm, loc.at[3])
            t_smem.start()
            t_smem.wait()
            h_local.wait()
            og_local.wait()
            remote(og_hbm.at[:, :, cols(c)], og.at[oc], ms.at[2], mr.at[2], other).wait_recv()
        remote(hid.at[oc, t], hid.at[oc, t], hcs.at[k], hcr.at[k], other).wait_recv()
        slots[k] = []
        for core in range(2):
            count = jnp.int32(0)
            index = [jnp.int32(0)] * CAP
            valid = [jnp.int32(0)] * CAP
            for b in range(BLOCKS):
                hit = (tsm[core, 0, b] == t).astype(jnp.int32)
                for r in range(CAP):
                    here = hit * (count == r).astype(jnp.int32)
                    index[r] = index[r] + b * here
                    valid[r] = valid[r] + here
                count = count + hit
            for r in range(CAP):
                slots[k].append((core, index[r]))
                rows = hid[core, t, r * BLOCK : (r + 1) * BLOCK, :].astype(F32) * valid[r].astype(F32)
                at = (core * CAP + r) * BLOCK
                hid_t[:, at : at + BLOCK] = rows.astype(BF16).T

    def weight_grad(k, g):
        t = wrap(x + k)
        width = GROUPS[g][0]

        def tile(j, carry):
            start = pl.multiple_of(j * TILE, TILE)
            rhs = jnp.concatenate(
                [og[core, i, :, pl.ds(OFFSETS[g] + start, TILE)] for core, i in slots[k]], axis=0
            )
            out = jnp.dot(hid_t[...], rhs, preferred_element_type=F32)
            part[g][t, :, :, :, pl.ds(start, TILE)] = out.astype(BF16).reshape(RING, RING, ROWS, TILE)
            return carry

        lax.fori_loop(0, width // TILE, tile, 0)

    def rows_of(who):
        return pl.ds(pl.multiple_of(who * (ROWS // 2), 8), ROWS // 2)

    def span_of(half, g):
        return pl.ds(pl.multiple_of(half * HALF, HALF) + OFFSETS[g], GROUPS[g][0])

    def fin_hop(g, half, rows):
        src = fin.at[rows_of(rows), OFFSETS[g] : OFFSETS[g] + GROUPS[g][0]]
        return (src, wgs.at[:, span_of(half, g)], fs.at[g], fr.at[g], other)

    def store(g, i, half):
        return pltpu.make_async_copy(wgs.at[:, span_of(half, g)], wg_hbm.at[:, span_of(half, g)], ws.at[i, g])

    def rs_copy(g, p, d, k, q, h):
        return remote(
            block(part[g], g, p, q, h),
            land[g][p].at[d, k],
            rs_s.at[g, p, d, k],
            rs_r.at[g, p, d, k],
            near(GROUPS[g][1][p], 1 - 2 * d),
        )

    def rs_send(*a):
        copy = rs_copy(*a)
        copy.start()
        sent.append(copy)

    def rs_direct(g, k, q):
        return remote(
            block(part[g], g, 0, q, None),
            land[g][0].at[k],
            rs_s.at[g, 0, 0, k],
            rs_r.at[g, 0, 0, k],
            near(GROUPS[g][1][0], DELTAS[k]),
        )

    def rs_start(g, p):
        m = mine[GROUPS[g][1][p]]
        if p < 2:
            rs_finish(g, p + 1)
        if p == 0:
            for k in range(3):
                copy = rs_direct(g, k, wrap(m + DELTAS[k]))
                copy.start()
                sent.append(copy)
            return
        for d in range(2):
            rs_send(g, p, d, 0, wrap(m + 2), d)
        for d in range(2):
            rs_send(g, p, d, 1, wrap(m + 1 - 2 * d), 1 - d)

    def add_in(g, p, q, h, parts):
        width, order = GROUPS[g]
        half = width // 2
        free = sorted(order[:p])
        span = pl.ds(h * half, half)

        def one(i, carry):
            lead = (i // RING, lax.rem(i, RING)) if p == 2 else (i,)
            at = list(mine)
            for axis, v in zip(free, lead):
                at[axis] = v
            at[order[p]] = q
            total = part[g][at[0], at[1], at[2], :, span].astype(F32)
            for d, k in parts:
                total = total + land[g][p][(d, k) + lead].astype(F32)
            part[g][at[0], at[1], at[2], :, span] = total.astype(BF16)
            return carry

        lax.fori_loop(0, RING**p, one, 0)

    def rs_middle(g, p):
        m = mine[GROUPS[g][1][p]]
        for d in range(2):
            q = wrap(m + 1 - 2 * d)
            rs_copy(g, p, d, 0, q, d).wait_recv()
            add_in(g, p, q, d, ((d, 0),))
            rs_send(g, p, d, 2, q, d)

    def rs_finish(g, p):
        m = mine[GROUPS[g][1][p]]
        if p == 0:
            total = part[g][mine].astype(F32)
            for k in range(3):
                rs_direct(g, k, m).wait_recv()
                total = total + land[g][0][k].astype(F32)
            fin[:, OFFSETS[g] : OFFSETS[g] + GROUPS[g][0]] = total
            push(*fin_hop(g, c, oc))
            wgs[:, span_of(c, g)] = fin[rows_of(c), OFFSETS[g] : OFFSETS[g] + GROUPS[g][0]]
            store(g, 0, c).start()
            return
        for k in (1, 2):
            for d in range(2):
                rs_copy(g, p, d, k, m, d if k == 2 else 1 - d).wait_recv()
        add_in(g, p, m, 0, ((0, 2), (1, 1)))
        add_in(g, p, m, 1, ((0, 1), (1, 2)))

    def half_product(k, b, groups):
        t = tsm[k, 0, b]
        acc = jnp.zeros((BLOCK, FF), F32)
        for g in groups:
            width = GROUPS[g][0]
            lhs = og[k, b, :, OFFSETS[g] : OFFSETS[g] + width]
            rhs = w[g][t].reshape(FF, width)
            acc = acc + lax.dot_general(lhs, rhs, (((1,), (1,)), ((), ())), preferred_element_type=F32)
        return acc

    def hidden_early(u):
        start = u * EARLY
        who, start = (oc, start) if start < BLOCKS else (c, start - BLOCKS)

        def one(b, carry):
            acc[who, b] = half_product(who, b, range(NG - LATE))
            return carry

        lax.fori_loop(start, start + EARLY, one, 0)

    def hidden_late(u):
        start = u * UNIT
        who, start = (oc, start) if start < BLOCKS else (c, start - BLOCKS)

        def one(b, carry):
            total = acc[who, b] + half_product(who, b, range(NG - LATE, NG))
            hop = remote(hsend.at[b], hrecv.at[b], hps.at[b], hpr.at[b], other)
            if u * UNIT < BLOCKS:
                hsend[b] = total.astype(BF16)
                hop.start()
            else:
                hop.wait_recv()
                hrecv[b] = ((total + hrecv[b].astype(F32)) * (D**-0.5)).astype(BF16)
                pltpu.make_async_copy(hrecv.at[b], hg_hbm.at[b], hos.at[b]).start()
            return carry

        lax.fori_loop(start, start + UNIT, one, 0)

    steps = {
        "as": ag_start,
        "af": ag_forward,
        "ae": ag_finish,
        "a2a": a2a,
        "hp": hid_push,
        "ht": take,
        "wg": weight_grad,
        "rs": rs_start,
        "rm": rs_middle,
        "re": rs_finish,
        "ha": hidden_early,
        "hb": hidden_late,
    }
    for name, *where in ORDER:
        steps[name](*where)

    ended = [where[0] for name, *where in ORDER if name == "re"]
    for g in ended:
        remote(*fin_hop(g, oc, c)).wait_recv()
        store(g, 1, oc).start()
    for g in ended:
        store(g, 0, c).wait()
        store(g, 1, oc).wait()

    def drain(b, carry):
        remote(hsend.at[b], hrecv.at[b], hps.at[b], hpr.at[b], other).wait_send()
        pltpu.make_async_copy(hrecv.at[b], hg_hbm.at[b], hos.at[b]).wait()
        return carry

    lax.fori_loop(0, BLOCKS, drain, 0)
    for copy in sent:
        copy.wait_send()


def exchange(out_grad, block_target, saved_hidden, master_weight):
    scratch = [pltpu.VMEM((1, BLOCKS), jnp.int32), pltpu.VMEM((2, BLOCKS, BLOCK, HALF), BF16)]
    for _ in range(2):
        scratch += [pltpu.VMEM((RING, RING, RING, ROWS, width), BF16) for width, _ in GROUPS]
    for width, _ in GROUPS:
        scratch += [pltpu.VMEM((3, ROWS, width), BF16)]
        scratch += [pltpu.VMEM((2, 3) + (RING,) * p + (ROWS, width // 2), BF16) for p in (1, 2)]
    dma = pltpu.SemaphoreType.DMA
    scratch += [
        pltpu.VMEM((2, EXPERTS, CAP * BLOCK, FF), BF16),
        pltpu.VMEM((FF, 2 * CAP * BLOCK), BF16),
        pltpu.VMEM((2, ROWS // 2, HALF), F32),
        pltpu.VMEM((2, BLOCKS, 128), jnp.int32),
        pltpu.SMEM((2, BLOCKS, 128), jnp.int32),
        pltpu.VMEM((BLOCKS, BLOCK, FF), BF16),
        pltpu.VMEM((BLOCKS, BLOCK, FF), BF16),
        pltpu.VMEM((2, BLOCKS, BLOCK, FF), F32),
        pltpu.VMEM((ROWS, HALF), F32),
        pltpu.VMEM((ROWS // 2, D), F32),
        dma((NG, 3, 2, 3)),
        dma((NG, 3, 2, 3)),
        dma((NG, 3, 2, 3)),
        dma((NG, 3, 2, 3)),
        dma((3,)),
        dma((3,)),
        dma((4,)),
        dma((4,)),
        dma((4,)),
        dma((4,)),
        dma((5,)),
        dma((BLOCKS,)),
        dma((BLOCKS,)),
        dma((BLOCKS,)),
        dma((NG,)),
        dma((NG,)),
        dma((2, NG)),
    ]
    anywhere = pl.BlockSpec(memory_space=pl.ANY)
    return pl.pallas_call(
        kernel,
        out_shape=(
            jax.ShapeDtypeStruct((BLOCKS, BLOCK, FF), BF16),
            jax.ShapeDtypeStruct((ROWS // 2, D), F32),
        ),
        in_specs=[anywhere] * 4,
        out_specs=(anywhere, anywhere),
        scratch_shapes=scratch,
        compiler_params=pltpu.CompilerParams(
            collective_id=0, has_side_effects=True, vmem_limit_bytes=63 * 1024 * 1024
        ),
        cost_estimate=pl.CostEstimate(flops=20 * 10**9, bytes_accessed=16 * 2**20, transcendentals=0),
    )(out_grad.reshape(BLOCKS, BLOCK, D), block_target.reshape(1, BLOCKS), saved_hidden, master_weight)


def body(out_grad, block_target, saved_hidden, master_weight, first_moment, second_moment):
    hidden, total = exchange(out_grad, block_target, saved_hidden, master_weight)
    hidden_grad = hidden.reshape(BLOCKS * BLOCK, FF)
    weight_grad = total[None] * (D**-0.5)
    new_first = BETA_ONE * first_moment + (1.0 - BETA_ONE) * weight_grad
    new_second = BETA_TWO * second_moment + (1.0 - BETA_TWO) * weight_grad * weight_grad
    first_fix = 1.0 - BETA_ONE**STEP
    second_fix = 1.0 - BETA_TWO**STEP
    new_weight = master_weight - LEARN_RATE * (new_first / first_fix) / (
        jnp.sqrt(new_second / second_fix) + EPSILON
    )
    return (hidden_grad, new_weight, new_first, new_second)


def solution(mesh):
    rows = P(("ep", "edp"), None)
    shard = P("ep", "edp", None)
    return jax.shard_map(
        body,
        mesh=mesh,
        in_specs=(rows, rows, rows, shard, shard, shard),
        out_specs=(rows, shard, shard, shard),
        check_vma=False,
    )
```
